256 devices in a mesh: pair: 2 (over x_hi), rows: 64 (over z, y, x_lo), cols: 2 (over core).
Axes of the slice: x: 4 (x_hi: 2, x_lo: 2; x = x_hi * 2 + x_lo), y: 4, z: 8, core: 2. Of those that a mesh axis runs over, the one named last changes fastest.
Arguments:
- source_image: bfloat16 [512, 512], P('rows', 'cols'), may hold values from -6 to 6
- target_images: bfloat16 [4, 512, 512], P('pair', 'rows', 'cols'), may hold values from -6 to 6
- prior_fields: float32 [4, 2, 512, 512], P('pair', None, 'rows', 'cols'), may hold values from -3 to 3
- offsets: int32 [4], P('pair'), may hold values from 0 to 2
- shift_lookup_matrix: bfloat16 [3, 128], replicated, may hold values from -6 to 6
- in_weight: bfloat16 [9, 2, 128], replicated, may hold values from -1.5 to 1.5
- in_bias: float32 [128], replicated, may hold values from -3 to 3
- hidden_weight: bfloat16 [2, 9, 128, 128], replicated, may hold values from -0.25 to 0.25
- hidden_bias: float32 [2, 128], replicated, may hold values from -2 to 2
- out_weight: bfloat16 [9, 2, 128], replicated, may hold values from -0.25 to 0.25
- out_bias: float32 [2], replicated, may hold values from -2 to 2
Outputs:
- candidates: float32 [4, 2, 512, 512], P('pair', None, 'rows', 'cols')
- voted: float32 [2, 512, 512], P(None, 'rows', 'cols')
The draws below stay inside these ranges and needn't reach their ends.
All inputs are finite; a program needn't handle non-finite values.
Results may differ from the reference program's by a relative error of at most 0.0084.
Values may be sent and summed in bfloat16 or wider, within the bound.
A program may use at most 64 MiB of HBM per device.

```python
import jax
import jax.numpy as jnp
from jax import lax

C = 128
HID = 2
OFFS = 3
K = 4
NR = 512
NC = 512


def place_ends(array, own_key, low, top_value):
    longest = array.shape.index(max(array.shape))
    spots = []
    for shift in (0, 1):
        where = [jax.random.randint(jax.random.fold_in(own_key, axis), (), 0, length) for axis, length in enumerate(array.shape)]
        where[longest] = (where[longest] + shift) % array.shape[longest]
        spots.append(tuple(where))
    return array.at[spots[0]].set(low).at[spots[1]].set(top_value)


def steps_of(rng, dims, pieces, low, largest):
    gain, own = 1.0, jax.random.fold_in(rng, 6)
    for axis_at, shards_of in pieces:
        heights = jnp.exp(jax.random.uniform(jax.random.fold_in(own, axis_at), (shards_of,), jnp.float32, low / len(pieces), largest / len(pieces)))
        gain = gain * jnp.repeat(heights, dims[axis_at] // shards_of).reshape([-1 if axis == axis_at else 1 for axis in range(len(dims))])
    return gain


def normal_values(key, extent, deviation, limit, split=(), dtype=jnp.bfloat16):
    drawn = jax.random.normal(key, extent, jnp.float32) * deviation
    if len(split) > 0:
        drawn = steps_of(key, extent, split, -0.22, 0.18) * drawn
    return jnp.clip(drawn, min=-limit, max=limit).astype(dtype)


def setup_inputs(seed: int = 0) -> dict:
    streams_of = jax.random.split(jax.random.key(seed), 12)
    return {
        "source_image": normal_values(streams_of[0], (NR, NC), 1.0, 6.0, ((0, 64), (1, 2))),
        "target_images": normal_values(streams_of[1], (K, NR, NC), 1.0, 6.0, ((0, 2), (1, 64), (2, 2))),
        "prior_fields": jnp.clip(jax.random.uniform(streams_of[2], (K, 2, NR, NC), jnp.float32, -3.0, 3.0) * steps_of(streams_of[2], (K, 2, NR, NC), ((0, 2), (2, 64), (3, 2)), -0.4, 0.0), -3.0, 3.0),
        "offsets": place_ends(jax.random.randint(streams_of[3], (K,), 0, OFFS), jax.random.fold_in(streams_of[3], 1), 0, OFFS - 1).astype(jnp.int32),
        "shift_lookup_matrix": normal_values(streams_of[4], (OFFS, C), 1.0, 6.0),
        "in_weight": normal_values(streams_of[5], (9, 2, C), 18 ** -0.5, 1.5),
        "in_bias": normal_values(streams_of[6], (C,), 0.5, 3.0, (), jnp.float32),
        "hidden_weight": normal_values(streams_of[7], (HID, 9, C, C), (9 * C // 2) ** -0.5, 0.25),
        "hidden_bias": normal_values(streams_of[8], (HID, C), 0.3, 2.0, (), jnp.float32),
        "out_weight": normal_values(streams_of[9], (9, 2, C), (9 * C // 2) ** -0.5, 0.25),
        "out_bias": normal_values(streams_of[10], (2,), 0.5, 2.0, (), jnp.float32),
    }


smoothing_sharpness = 4.0
max_shift = 2.0


def conv_input(padded, weight):
    rows_out = padded.shape[1] - 2
    cols_out = padded.shape[2] - 2
    total = jnp.zeros((rows_out, cols_out, weight.shape[2]), jnp.float32)
    for position in range(9):
        window = padded[:, position // 3:position // 3 + rows_out, position % 3:position % 3 + cols_out]
        total = total + jnp.einsum("erw,ed->rwd", window.astype(jnp.float32), weight[position].astype(jnp.float32))
    return total


def conv_hidden(padded, weight, offset_term):
    rows_out = padded.shape[0] - 2
    cols_out = padded.shape[1] - 2
    width = weight.shape[2]
    total = jnp.zeros((rows_out * cols_out, width), jnp.float32)
    for position in range(9):
        window = padded[position // 3:position // 3 + rows_out, position % 3:position % 3 + cols_out, :]
        total = total + jnp.dot(window.reshape(rows_out * cols_out, width), weight[position], preferred_element_type=jnp.float32)
    return total.reshape(rows_out, cols_out, width) + offset_term


def conv_output(padded, weight):
    rows_out = padded.shape[0] - 2
    cols_out = padded.shape[1] - 2
    width = padded.shape[2]
    total = jnp.zeros((rows_out * cols_out, 2), jnp.float32)
    for position in range(9):
        window = padded[position // 3:position // 3 + rows_out, position % 3:position % 3 + cols_out, :]
        total = total + jnp.dot(window.reshape(rows_out * cols_out, width), weight[position].T, preferred_element_type=jnp.float32)
    return total.reshape(rows_out, cols_out, 2).transpose(2, 0, 1)


def elect_consensus_flows(cands):
    number_of_flows = cands.shape[0]
    differ = cands[:, None] - cands[None, :]
    mutual_separation = jnp.sum(differ * differ, axis=2)
    ballot_weighting = jnp.sum(mutual_separation, axis=1) / ((number_of_flows - 1) * smoothing_sharpness)
    expo = jnp.exp(-ballot_weighting)
    weight = expo / jnp.sum(expo, axis=0)
    return jnp.sum(weight[:, None] * cands, axis=0)


def reference(source_image, target_images, prior_fields, offsets, shift_lookup_matrix, in_weight, in_bias, hidden_weight, hidden_bias, out_weight, out_bias):
    rows_total, cols_total = source_image.shape

    def single_couple(items):
        target, prior, offset = items
        stacked_fields = jnp.pad(jnp.stack([source_image, target]), ((0, 0), (1, 1), (1, 1)))
        embed = shift_lookup_matrix[offset].astype(jnp.float32)
        hidden = jax.nn.relu(conv_input(stacked_fields, in_weight) + in_bias + embed).astype(jnp.bfloat16)
        for layer in range(HID):
            padded = jnp.pad(hidden, ((1, 1), (1, 1), (0, 0)))
            hidden = jax.nn.relu(conv_hidden(padded, hidden_weight[layer], hidden_bias[layer])).astype(jnp.bfloat16)
        padded = jnp.pad(hidden, ((1, 1), (1, 1), (0, 0)))
        flow_field = max_shift * jnp.tanh(conv_output(padded, out_weight) + out_bias[:, None, None])
        row_pos = jnp.arange(rows_total).astype(jnp.float32)[:, None] + flow_field[0]
        col_pos = jnp.arange(cols_total).astype(jnp.float32)[None, :] + flow_field[1]
        row_floor = jnp.floor(row_pos)
        col_floor = jnp.floor(col_pos)
        row_frac = row_pos - row_floor
        col_frac = col_pos - col_floor
        row_index = row_floor.astype(jnp.int32) + 3
        col_index = col_floor.astype(jnp.int32) + 3
        prior_padded = jnp.pad(prior, ((0, 0), (3, 3), (3, 3)))
        upper_left = prior_padded[:, row_index, col_index]
        upper_right = prior_padded[:, row_index, col_index + 1]
        lower_left = prior_padded[:, row_index + 1, col_index]
        lower_right = prior_padded[:, row_index + 1, col_index + 1]
        sampled = ((1.0 - row_frac) * (1.0 - col_frac) * upper_left + (1.0 - row_frac) * col_frac * upper_right
                   + row_frac * (1.0 - col_frac) * lower_left + row_frac * col_frac * lower_right)
        return flow_field + sampled

    candidates = lax.map(single_couple, (target_images, prior_fields, offsets))
    return candidates, elect_consensus_flows(candidates)
```

```python
import functools

import jax
import jax.numpy as jnp
from jax import lax
from jax.experimental import pallas as pl
from jax.experimental.pallas import tpu as pltpu
from jax.sharding import PartitionSpec as P

MESH = pl.DeviceIdType.MESH
BF = jnp.bfloat16
F32 = jnp.float32

sharpness = 4.0
max_shift = 2.0
OFF = -1e30

Q = 16
STRIDE = 17
ROWS_M = STRIDE * Q
ROWS_X = (STRIDE + 2) * Q
RING = 384


def dot(a, b, dims=((1,), (0,))):
    return lax.dot_general(a, b, (dims, ((), ())), preferred_element_type=F32)


def store_slabs(ref, index, y):
    ref[index, 0:ROWS_M, :] = y.astype(BF)
    first = pltpu.roll(y[0:Q], Q - 1, 0)
    second = pltpu.roll(y[Q : 2 * Q], Q - 1, 0)
    ref[index, ROWS_M:ROWS_X, :] = jnp.concatenate([first, second], axis=0).astype(BF)


def kernel(
    n_rows,
    src_ref,
    tgt_ref,
    prior_ref,
    off_ref,
    table_ref,
    inw_ref,
    inb_ref,
    hw_ref,
    hb_ref,
    outw_ref,
    outb_ref,
    cand_ref,
    vote_ref,
    img,
    side,
    pri,
    wts,
    pmat,
    qmat,
    gin,
    toe,
    gout,
    wout,
    feat,
    hid1,
    hid2,
    masks,
    every,
    w_sem,
    p_sem,
    img_send,
    img_recv,
    pri_send,
    pri_recv,
    cand_send,
    cand_recv,
):
    pair = lax.axis_index("pair")
    row = lax.axis_index("rows")
    col = lax.axis_index("cols")
    up = lax.rem(row + n_rows - 1, n_rows)
    down = lax.rem(row + 1, n_rows)
    other = 1 - col
    partner = 1 - pair
    tile_rows = 8
    rows_all = n_rows * tile_rows
    places = (
        (pair, up, col),
        (pair, down, col),
        (pair, row, other),
        (pair, up, other),
        (pair, down, other),
    )

    barrier = pltpu.get_barrier_semaphore()
    for place in places + ((partner, row, col),):
        pl.semaphore_signal(barrier, inc=1, device_id=place, device_id_type=MESH)

    weight_copies = []
    for number, (a, where, r0, l0) in enumerate(
        ((0, 0, 0, 0), (1, 0, 128, 0), (0, 0, 128, 128), (2, 1, 0, 0), (1, 1, 0, 128), (2, 1, 128, 128))
    ):
        copy = pltpu.make_async_copy(
            hw_ref.at[:, pl.ds(3 * a, 3)],
            wts.at[:, :, where, pl.ds(r0, 128), pl.ds(l0, 128)],
            w_sem.at[number],
        )
        copy.start()
        weight_copies.append(copy)
    own_prior = pltpu.make_async_copy(
        prior_ref, pri.at[:, :, pl.ds(8, 8), pl.ds(0, 256)], p_sem
    )
    own_prior.start()

    src = src_ref[...].astype(F32)
    tgt = tgt_ref[...].astype(F32)
    own = jnp.concatenate([src, tgt[0], tgt[1], jnp.zeros_like(src)], axis=0).astype(BF)
    img[0, :, 0:256] = own
    side[...] = jnp.where(col == 0, own[:, 128:256], own[:, 0:128])

    pl.semaphore_wait(barrier, 6)

    main = pl.ds(0, 256)
    edge = pl.ds(256, 128)
    routes = ((2, main), (1, main), (0, edge), (2, edge), (1, edge))
    image_copies = []
    for number, (slot, lanes) in enumerate(routes):
        copy = pltpu.make_async_remote_copy(
            src_ref=img.at[0, :, main] if number < 2 else side,
            dst_ref=img.at[slot, :, lanes],
            send_sem=img_send.at[number],
            recv_sem=img_recv.at[number],
            device_id=places[number],
            device_id_type=MESH,
        )
        copy.start()
        image_copies.append(copy)
    half = pl.ds(pl.multiple_of((1 - col) * 128, 128), 128)
    prior_copies = []
    for number, (slot, lanes) in enumerate(routes):
        start = (8, 0, 16)[slot]
        copy = pltpu.make_async_remote_copy(
            src_ref=prior_ref if number < 2 else prior_ref.at[:, :, :, half],
            dst_ref=pri.at[:, :, pl.ds(start, 8), lanes],
            send_sem=pri_send.at[number],
            recv_sem=pri_recv.at[number],
            device_id=places[number],
            device_id_type=MESH,
        )
        copy.start()
        prior_copies.append(copy)

    slab = lax.broadcasted_iota(jnp.int32, (STRIDE + 2, Q, RING), 0)
    chunk = lax.broadcasted_iota(jnp.int32, (STRIDE + 2, Q, RING), 1)
    lane = lax.broadcasted_iota(jnp.int32, (STRIDE + 2, Q, RING), 2)
    at = chunk * STRIDE + slab
    place = at - 4
    place = jnp.where(place < 0, place + RING, place)
    pmat[...] = jnp.where(place == lane, 1.0, 0.0).reshape(ROWS_X, RING).astype(BF)
    qmat[...] = jnp.where(at == lane, 1.0, 0.0).reshape(ROWS_X, RING)[0:ROWS_M].astype(BF)

    m_slab = lax.broadcasted_iota(jnp.int32, (7, Q, 256), 0)
    m_chunk = lax.broadcasted_iota(jnp.int32, (7, Q, 256), 1)
    m_at = m_chunk * STRIDE + m_slab + col * 256
    for layer in range(3):
        inside = (m_at >= 3 - layer) & (m_at < 512 + 3 - layer)
        masks[layer] = jnp.where(inside, 1.0, 0.0).reshape(7 * Q, 256)

    gin[...] = jnp.zeros_like(gin)
    for b in range(3):
        for ch in range(2):
            for a in range(3):
                w = inw_ref[3 * a + b, ch : ch + 1, :].astype(F32)
                gin[2 * b + ch, a : a + 1, :] = w
                gin[2 * b + ch, 16 + a : 17 + a, :] = w
    for r in range(14):
        start = (20 - r) % 16
        block = jnp.concatenate(
            [gin[g, start : start + 16, :] for g in range(6)] + [jnp.zeros((32, 128), F32)], axis=0
        )
        toe[:, r * 128 : (r + 1) * 128] = block.astype(BF)

    gout[...] = jnp.zeros_like(gout)
    for b in range(3):
        for e in range(2):
            for a in range(3):
                gout[2 * b + e, 10 - a : 11 - a, :] = outw_ref[3 * a + b, e : e + 1, :].astype(F32)
    for p in range(5):
        for h in range(2):
            start = 10 - (2 * p + h)
            block = jnp.concatenate([gout[g, start : start + 8, :] for g in range(6)], axis=0)
            wout[:, p * 256 + h * 128 : p * 256 + (h + 1) * 128] = block.astype(BF)

    for layer in range(2):
        for b in range(3):
            wts[layer, b, 0, 0:128, 128:256] = jnp.zeros((128, 128), BF)
            wts[layer, b, 1, 128:256, 0:128] = jnp.zeros((128, 128), BF)

    for copy in image_copies:
        copy.wait_recv()

    lane8 = lax.broadcasted_iota(jnp.int32, (8, RING), 1)
    sub8 = lax.broadcasted_iota(jnp.int32, (8, RING), 0)
    lanes_ok = (lane8 < 256) | ((lane8 < 320) == (col == 0))
    above_ok = jnp.logical_and(lanes_ok, row > 0)
    below_ok = jnp.logical_and(lanes_ok, row < n_rows - 1)
    tiles = [img[t].astype(F32) for t in range(3)]
    parts = []
    for s in range(3):
        mine, above, below = (t[8 * s : 8 * s + 8] for t in tiles)
        parts.append(jnp.where(lanes_ok, mine, 0.0))
        parts.append(
            jnp.where(sub8 < 4, jnp.where(below_ok, below, 0.0), jnp.where(above_ok, above, 0.0))
        )
    blank = jnp.zeros((96, RING), F32)
    stack = jnp.concatenate(
        [parts[0], parts[1], parts[2], parts[3], blank, parts[0], parts[1], parts[4], parts[5], blank],
        axis=0,
    ).astype(BF)
    cols_in = dot(pmat[...], stack, ((1,), (1,)))

    def row_bias(bias, first_row):
        which = first_row + lax.broadcasted_iota(jnp.int32, (1, 256), 1) // 128
        return jnp.where((which >= 0) & (which < rows_all), bias, OFF)

    def twice(vector):
        return jnp.concatenate([vector, vector], axis=1)

    def finish(total, bias, layer):
        y = jnp.maximum(total + bias, 0.0)
        return jnp.concatenate([y[0 : 7 * Q] * masks[layer], y[7 * Q :]], axis=0)

    def hidden(source, target, layer, count, bias, above):
        @pl.loop(0, count)
        def _(p):
            total = None
            for b in range(3):
                for where in range(2):
                    term = dot(source[p + where, b * Q : b * Q + ROWS_M, :], wts[layer, b, where])
                    total = term if total is None else total + term
            bias_here = row_bias(bias, row * tile_rows + 2 * p - above)
            store_slabs(target, p, finish(total, bias_here, layer + 1))

    table = table_ref[...].astype(F32)
    in_bias = inb_ref[...].reshape(1, 128)
    hidden_bias = hb_ref[...]
    for copy in weight_copies:
        copy.wait()

    for k in range(2):
        here = cols_in[:, 128 * k : 128 * k + 128]
        lhs = (
            here[0:ROWS_M]
            + pltpu.roll(here[Q : Q + ROWS_M], 32, 1)
            + pltpu.roll(here[2 * Q : 2 * Q + ROWS_M], 64, 1)
        ).astype(BF)
        embed = jnp.zeros((1, 128), F32)
        for o in range(table.shape[0]):
            embed = embed + jnp.where(off_ref[k] == o, table[o : o + 1], 0.0)
        bias = twice(in_bias + embed)
        for p in range(7):
            total = dot(lhs, toe[:, p * 256 : (p + 1) * 256])
            bias_here = row_bias(bias, row * tile_rows + 2 * p - 3)
            store_slabs(feat, p, finish(total, bias_here, 0))
        hidden(feat, hid1, 0, 6, twice(hidden_bias[0:1]), 2)
        hidden(hid1, hid2, 1, 5, twice(hidden_bias[1:2]), 1)

        flat = None
        for p in range(5):
            term = dot(wout[:, p * 256 : (p + 1) * 256], hid2[p, 0:ROWS_M, :], ((1,), (1,)))
            flat = term if flat is None else flat + term
        high = flat.astype(BF)
        rest = flat - high.astype(F32)
        mid = rest.astype(BF)
        low = (rest - mid.astype(F32)).astype(BF)
        pieces = dot(jnp.concatenate([high, mid, low], axis=0), qmat[...])
        natural = pieces[0:48] + pieces[48:96] + pieces[96:144]
        if k == 0:
            for copy in prior_copies:
                copy.wait_recv()
            own_prior.wait()
            keep = lanes_ok
            for pp in range(2):
                for e in range(2):
                    pri[pp, e, 0:8, :] = jnp.where(above_ok, pri[pp, e, 0:8, :], 0.0)
                    pri[pp, e, 8:16, :] = jnp.where(keep, pri[pp, e, 8:16, :], 0.0)
                    pri[pp, e, 16:24, :] = jnp.where(below_ok, pri[pp, e, 16:24, :], 0.0)
        flow = []
        for e in range(2):
            z0 = natural[8 * e : 8 * e + 8]
            z1 = pltpu.roll(natural[16 + 8 * e : 24 + 8 * e], RING - 1, 1)
            z2 = pltpu.roll(natural[32 + 8 * e : 40 + 8 * e], RING - 2, 1)
            flow.append(max_shift * jnp.tanh((z0 + z1 + z2)[:, 0:256] + outb_ref[e]))
        row_weight = [jnp.maximum(1.0 - jnp.abs(flow[0] - s), 0.0) for s in range(-2, 3)]
        col_weight = [jnp.maximum(1.0 - jnp.abs(flow[1] - s), 0.0) for s in range(-2, 3)]
        mine = pair * 2 + k
        for e in range(2):
            value = flow[e]
            for rs in range(-2, 3):
                band = pri[k, e, 8 + rs : 16 + rs, :]
                inner = None
                for cs in range(-2, 3):
                    moved = band if cs == 0 else pltpu.roll(band, (RING - cs) % RING, 1)
                    term = col_weight[cs + 2] * moved[:, 0:256]
                    inner = term if inner is None else inner + term
                value = value + row_weight[rs + 2] * inner
            cand_ref[k, e] = value
            every[mine, e] = value
        copy = pltpu.make_async_remote_copy(
            src_ref=every.at[mine],
            dst_ref=every.at[mine],
            send_sem=cand_send.at[k],
            recv_sem=cand_recv.at[k],
            device_id=(partner, row, col),
            device_id_type=MESH,
        )
        copy.start()
        if k == 0:
            first_copy = copy
        else:
            second_copy = copy

    first_copy.wait()
    second_copy.wait()
    c = [[every[k, e] for e in range(2)] for k in range(4)]
    score = [None] * 4
    for i in range(4):
        for j in range(i + 1, 4):
            dr = c[i][0] - c[j][0]
            dc = c[i][1] - c[j][1]
            apart = dr * dr + dc * dc
            score[i] = apart if score[i] is None else score[i] + apart
            score[j] = apart if score[j] is None else score[j] + apart
    weight = [jnp.exp(score[i] * (-1.0 / (3 * sharpness))) for i in range(4)]
    bottom = (weight[0] + weight[1]) + (weight[2] + weight[3])
    for e in range(2):
        top = (weight[0] * c[0][e] + weight[1] * c[1][e]) + (
            weight[2] * c[2][e] + weight[3] * c[3][e]
        )
        vote_ref[e] = top / bottom

    for copy in image_copies + prior_copies:
        copy.wait_send()


def solution(mesh):
    n_rows = mesh.shape["rows"]
    in_specs = (
        P("rows", "cols"),
        P("pair", "rows", "cols"),
        P("pair", None, "rows", "cols"),
        P("pair"),
        P(),
        P(),
        P(),
        P(),
        P(),
        P(),
        P(),
    )
    out_specs = (P("pair", None, "rows", "cols"), P(None, "rows", "cols"))
    vmem = pl.BlockSpec(memory_space=pltpu.VMEM)
    smem = pl.BlockSpec(memory_space=pltpu.SMEM)
    anywhere = pl.BlockSpec(memory_space=pl.ANY)
    dma = pltpu.SemaphoreType.DMA

    def shards(*args):
        return pl.pallas_call(
            functools.partial(kernel, n_rows),
            out_shape=(
                jax.ShapeDtypeStruct((2, 2, 8, 256), F32),
                jax.ShapeDtypeStruct((2, 8, 256), F32),
            ),
            in_specs=[vmem, vmem, anywhere, smem, vmem, vmem, vmem, anywhere, vmem, vmem, smem],
            out_specs=(vmem, vmem),
            scratch_shapes=[
                pltpu.VMEM((3, 32, RING), BF),
                pltpu.VMEM((32, 128), BF),
                pltpu.VMEM((2, 2, 24, RING), F32),
                pltpu.VMEM((2, 3, 2, 256, 256), BF),
                pltpu.VMEM((ROWS_X, RING), BF),
                pltpu.VMEM((ROWS_M, RING), BF),
                pltpu.VMEM((6, 32, 128), F32),
                pltpu.VMEM((128, 14 * 128), BF),
                pltpu.VMEM((6, 24, 128), F32),
                pltpu.VMEM((48, 5 * 256), BF),
                pltpu.VMEM((7, ROWS_X, 256), BF),
                pltpu.VMEM((6, ROWS_X, 256), BF),
                pltpu.VMEM((5, ROWS_X, 256), BF),
                pltpu.VMEM((3, 7 * Q, 256), F32),
                pltpu.VMEM((4, 2, 8, 256), F32),
                dma((6,)),
                dma,
                dma((5,)),
                dma((5,)),
                dma((5,)),
                dma((5,)),
                dma((2,)),
                dma((2,)),
            ],
            compiler_params=pltpu.CompilerParams(
                collective_id=0, has_side_effects=True, vmem_limit_bytes=32 * 1024 * 1024
            ),
        )(*args)

    return jax.shard_map(shards, mesh=mesh, in_specs=in_specs, out_specs=out_specs, check_vma=False)
```

```python
import functools

import jax
import jax.numpy as jnp
from jax import lax
from jax.experimental import pallas as pl
from jax.experimental.pallas import tpu as pltpu
from jax.sharding import PartitionSpec as P

MESH = pl.DeviceIdType.MESH
BF = jnp.bfloat16
F32 = jnp.float32

sharpness = 4.0
max_shift = 2.0
OFF = -1e30

Q = 16
STRIDE = 17
ROWS_M = STRIDE * Q
ROWS_X = (STRIDE + 2) * Q
RING = 384


def dot(a, b, dims=((1,), (0,))):
    return lax.dot_general(a, b, (dims, ((), ())), preferred_element_type=F32)


def store_slabs(ref, index, y):
    ref[index, 0:ROWS_M, :] = y.astype(BF)
    first = pltpu.roll(y[0:Q], Q - 1, 0)
    second = pltpu.roll(y[Q : 2 * Q], Q - 1, 0)
    ref[index, ROWS_M:ROWS_X, :] = jnp.concatenate([first, second], axis=0).astype(BF)


def kernel(
    n_rows,
    src_in,
    tgt_in,
    prior_ref,
    off_in,
    table_in,
    inw_in,
    inb_in,
    hw_ref,
    hb_in,
    outw_in,
    outb_in,
    every,
    src_ref,
    tgt_ref,
    off_ref,
    table_ref,
    inw_ref,
    inb_ref,
    hb_ref,
    outw_ref,
    outb_ref,
    img,
    side,
    pri,
    wts,
    pmat,
    qmat,
    gin,
    toe,
    gout,
    wout,
    feat,
    hid1,
    hid2,
    masks,
    in_sem,
    w_sem,
    p_sem,
    img_send,
    img_recv,
    pri_send,
    pri_recv,
    cand_send,
    cand_recv,
):
    pair = lax.axis_index("pair")
    row = lax.axis_index("rows")
    col = lax.axis_index("cols")
    up = lax.rem(row + n_rows - 1, n_rows)
    down = lax.rem(row + 1, n_rows)
    other = 1 - col
    partner = 1 - pair
    tile_rows = 8
    rows_all = n_rows * tile_rows
    places = (
        (pair, up, col),
        (pair, down, col),
        (pair, row, other),
        (pair, up, other),
        (pair, down, other),
    )

    barrier = pltpu.get_barrier_semaphore()
    for place in places + ((partner, row, col),):
        pl.semaphore_signal(barrier, inc=1, device_id=place, device_id_type=MESH)

    loads = []
    for number, (source, target) in enumerate(
        (
            (src_in, src_ref),
            (tgt_in, tgt_ref),
            (inw_in, inw_ref),
            (outw_in, outw_ref),
            (off_in, off_ref),
            (table_in, table_ref),
            (inb_in, inb_ref),
            (hb_in, hb_ref),
            (outb_in, outb_ref),
        )
    ):
        copy = pltpu.make_async_copy(source, target, in_sem.at[number])
        copy.start()
        loads.append(copy)

    weight_copies = []
    for number, (a, where, r0, l0) in enumerate(
        ((0, 0, 0, 0), (1, 0, 128, 0), (0, 0, 128, 128), (2, 1, 0, 0), (1, 1, 0, 128), (2, 1, 128, 128))
    ):
        copy = pltpu.make_async_copy(
            hw_ref.at[:, pl.ds(3 * a, 3)],
            wts.at[:, :, where, pl.ds(r0, 128), pl.ds(l0, 128)],
            w_sem.at[number],
        )
        copy.start()
        weight_copies.append(copy)
    own_prior = pltpu.make_async_copy(
        prior_ref, pri.at[:, :, pl.ds(8, 8), pl.ds(0, 256)], p_sem
    )
    own_prior.start()

    for copy in loads[:2]:
        copy.wait()
    src = src_ref[...].astype(F32)
    tgt = tgt_ref[...].astype(F32)
    own = jnp.concatenate([src, tgt[0], tgt[1], jnp.zeros_like(src)], axis=0).astype(BF)
    img[0, :, 0:256] = own
    side[...] = jnp.where(col == 0, own[:, 128:256], own[:, 0:128])

    pl.semaphore_wait(barrier, 6)

    main = pl.ds(0, 256)
    edge = pl.ds(256, 128)
    routes = ((2, main), (1, main), (0, edge), (2, edge), (1, edge))
    image_copies = []
    for number, (slot, lanes) in enumerate(routes):
        copy = pltpu.make_async_remote_copy(
            src_ref=img.at[0, :, main] if number < 2 else side,
            dst_ref=img.at[slot, :, lanes],
            send_sem=img_send.at[number],
            recv_sem=img_recv.at[number],
            device_id=places[number],
            device_id_type=MESH,
        )
        copy.start()
        image_copies.append(copy)
    half = pl.ds(pl.multiple_of((1 - col) * 128, 128), 128)
    prior_copies = []
    for number, (slot, lanes) in enumerate(routes):
        start = (8, 0, 16)[slot]
        copy = pltpu.make_async_remote_copy(
            src_ref=prior_ref if number < 2 else prior_ref.at[:, :, :, half],
            dst_ref=pri.at[:, :, pl.ds(start, 8), lanes],
            send_sem=pri_send.at[number],
            recv_sem=pri_recv.at[number],
            device_id=places[number],
            device_id_type=MESH,
        )
        copy.start()
        prior_copies.append(copy)

    slab = lax.broadcasted_iota(jnp.int32, (STRIDE + 2, Q, RING), 0)
    chunk = lax.broadcasted_iota(jnp.int32, (STRIDE + 2, Q, RING), 1)
    lane = lax.broadcasted_iota(jnp.int32, (STRIDE + 2, Q, RING), 2)
    at = chunk * STRIDE + slab
    place = at - 4
    place = jnp.where(place < 0, place + RING, place)
    pmat[...] = jnp.where(place == lane, 1.0, 0.0).reshape(ROWS_X, RING).astype(BF)
    qmat[...] = jnp.where(at == lane, 1.0, 0.0).reshape(ROWS_X, RING)[0:ROWS_M].astype(BF)

    m_slab = lax.broadcasted_iota(jnp.int32, (7, Q, 256), 0)
    m_chunk = lax.broadcasted_iota(jnp.int32, (7, Q, 256), 1)
    m_at = m_chunk * STRIDE + m_slab + col * 256
    for layer in range(3):
        inside = (m_at >= 3 - layer) & (m_at < 512 + 3 - layer)
        masks[layer] = jnp.where(inside, 1.0, 0.0).reshape(7 * Q, 256)

    for copy in loads[2:]:
        copy.wait()
    gin[...] = jnp.zeros_like(gin)
    for b in range(3):
        for ch in range(2):
            for a in range(3):
                w = inw_ref[3 * a + b, ch : ch + 1, :].astype(F32)
                gin[2 * b + ch, a : a + 1, :] = w
                gin[2 * b + ch, 16 + a : 17 + a, :] = w
    for r in range(14):
        start = (20 - r) % 16
        block = jnp.concatenate(
            [gin[g, start : start + 16, :] for g in range(6)] + [jnp.zeros((32, 128), F32)], axis=0
        )
        toe[:, r * 128 : (r + 1) * 128] = block.astype(BF)

    gout[...] = jnp.zeros_like(gout)
    for b in range(3):
        for e in range(2):
            for a in range(3):
                gout[2 * b + e, 10 - a : 11 - a, :] = outw_ref[3 * a + b, e : e + 1, :].astype(F32)
    for p in range(5):
        for h in range(2):
            start = 10 - (2 * p + h)
            block = jnp.concatenate([gout[g, start : start + 8, :] for g in range(6)], axis=0)
            wout[:, p * 256 + h * 128 : p * 256 + (h + 1) * 128] = block.astype(BF)

    for layer in range(2):
        for b in range(3):
            wts[layer, b, 0, 0:128, 128:256] = jnp.zeros((128, 128), BF)
            wts[layer, b, 1, 128:256, 0:128] = jnp.zeros((128, 128), BF)

    for copy in image_copies:
        copy.wait_recv()

    lane8 = lax.broadcasted_iota(jnp.int32, (8, RING), 1)
    sub8 = lax.broadcasted_iota(jnp.int32, (8, RING), 0)
    lanes_ok = (lane8 < 256) | ((lane8 < 320) == (col == 0))
    above_ok = jnp.logical_and(lanes_ok, row > 0)
    below_ok = jnp.logical_and(lanes_ok, row < n_rows - 1)
    tiles = [img[t].astype(F32) for t in range(3)]
    parts = []
    for s in range(3):
        mine, above, below = (t[8 * s : 8 * s + 8] for t in tiles)
        parts.append(jnp.where(lanes_ok, mine, 0.0))
        parts.append(
            jnp.where(sub8 < 4, jnp.where(below_ok, below, 0.0), jnp.where(above_ok, above, 0.0))
        )
    blank = jnp.zeros((96, RING), F32)
    stack = jnp.concatenate(
        [parts[0], parts[1], parts[2], parts[3], blank, parts[0], parts[1], parts[4], parts[5], blank],
        axis=0,
    ).astype(BF)
    cols_in = dot(pmat[...], stack, ((1,), (1,)))

    def row_bias(bias, first_row):
        which = first_row + lax.broadcasted_iota(jnp.int32, (1, 256), 1) // 128
        return jnp.where((which >= 0) & (which < rows_all), bias, OFF)

    def twice(vector):
        return jnp.concatenate([vector, vector], axis=1)

    def finish(total, bias, layer):
        y = jnp.maximum(total + bias, 0.0)
        return jnp.concatenate([y[0 : 7 * Q] * masks[layer], y[7 * Q :]], axis=0)

    def hidden(source, target, layer, count, bias, above):
        @pl.loop(0, count, unroll=count)
        def _(p):
            total = None
            for b in range(3):
                for where in range(2):
                    term = dot(source[p + where, b * Q : b * Q + ROWS_M, :], wts[layer, b, where])
                    total = term if total is None else total + term
            bias_here = row_bias(bias, row * tile_rows + 2 * p - above)
            store_slabs(target, p, finish(total, bias_here, layer + 1))

    table = table_ref[...].astype(F32)
    in_bias = inb_ref[...].reshape(1, 128)
    hidden_bias = hb_ref[...]
    for copy in weight_copies:
        copy.wait()

    for k in range(2):
        here = cols_in[:, 128 * k : 128 * k + 128]
        lhs = (
            here[0:ROWS_M]
            + pltpu.roll(here[Q : Q + ROWS_M], 32, 1)
            + pltpu.roll(here[2 * Q : 2 * Q + ROWS_M], 64, 1)
        ).astype(BF)
        embed = jnp.zeros((1, 128), F32)
        for o in range(table.shape[0]):
            embed = embed + jnp.where(off_ref[k] == o, table[o : o + 1], 0.0)
        bias = twice(in_bias + embed)
        for p in range(7):
            total = dot(lhs, toe[:, p * 256 : (p + 1) * 256])
            bias_here = row_bias(bias, row * tile_rows + 2 * p - 3)
            store_slabs(feat, p, finish(total, bias_here, 0))
        hidden(feat, hid1, 0, 6, twice(hidden_bias[0:1]), 2)
        hidden(hid1, hid2, 1, 5, twice(hidden_bias[1:2]), 1)

        flat = None
        for p in range(5):
            term = dot(wout[:, p * 256 : (p + 1) * 256], hid2[p, 0:ROWS_M, :], ((1,), (1,)))
            flat = term if flat is None else flat + term
        high = flat.astype(BF)
        rest = flat - high.astype(F32)
        mid = rest.astype(BF)
        low = (rest - mid.astype(F32)).astype(BF)
        pieces = dot(jnp.concatenate([high, mid, low], axis=0), qmat[...])
        natural = pieces[0:48] + pieces[48:96] + pieces[96:144]
        if k == 0:
            for copy in prior_copies:
                copy.wait_recv()
            own_prior.wait()
            keep = lanes_ok
            for pp in range(2):
                for e in range(2):
                    pri[pp, e, 0:8, :] = jnp.where(above_ok, pri[pp, e, 0:8, :], 0.0)
                    pri[pp, e, 8:16, :] = jnp.where(keep, pri[pp, e, 8:16, :], 0.0)
                    pri[pp, e, 16:24, :] = jnp.where(below_ok, pri[pp, e, 16:24, :], 0.0)
        flow = []
        for e in range(2):
            z0 = natural[8 * e : 8 * e + 8]
            z1 = pltpu.roll(natural[16 + 8 * e : 24 + 8 * e], RING - 1, 1)
            z2 = pltpu.roll(natural[32 + 8 * e : 40 + 8 * e], RING - 2, 1)
            flow.append(max_shift * jnp.tanh((z0 + z1 + z2)[:, 0:256] + outb_ref[e]))
        row_weight = [jnp.maximum(1.0 - jnp.abs(flow[0] - s), 0.0) for s in range(-2, 3)]
        col_weight = [jnp.maximum(1.0 - jnp.abs(flow[1] - s), 0.0) for s in range(-2, 3)]
        mine = pair * 2 + k
        for e in range(2):
            value = flow[e]
            for rs in range(-2, 3):
                band = pri[k, e, 8 + rs : 16 + rs, :]
                inner = None
                for cs in range(-2, 3):
                    moved = band if cs == 0 else pltpu.roll(band, (RING - cs) % RING, 1)
                    term = col_weight[cs + 2] * moved[:, 0:256]
                    inner = term if inner is None else inner + term
                value = value + row_weight[rs + 2] * inner
            every[mine, e] = value
        copy = pltpu.make_async_remote_copy(
            src_ref=every.at[mine],
            dst_ref=every.at[mine],
            send_sem=cand_send.at[k],
            recv_sem=cand_recv.at[k],
            device_id=(partner, row, col),
            device_id_type=MESH,
        )
        copy.start()
        if k == 0:
            first_copy = copy
        else:
            second_copy = copy

    first_copy.wait()
    second_copy.wait()
    for copy in image_copies + prior_copies:
        copy.wait_send()


def vote(every, cand_ref, vote_ref):
    pair = lax.axis_index("pair")
    for k in range(2):
        cand_ref[k] = every[2 * pair + k]
    c = [[every[k, e] for e in range(2)] for k in range(4)]
    score = [None] * 4
    for i in range(4):
        for j in range(i + 1, 4):
            dr = c[i][0] - c[j][0]
            dc = c[i][1] - c[j][1]
            apart = dr * dr + dc * dc
            score[i] = apart if score[i] is None else score[i] + apart
            score[j] = apart if score[j] is None else score[j] + apart
    weight = [jnp.exp(score[i] * (-1.0 / (3 * sharpness))) for i in range(4)]
    bottom = (weight[0] + weight[1]) + (weight[2] + weight[3])
    for e in range(2):
        top = (weight[0] * c[0][e] + weight[1] * c[1][e]) + (
            weight[2] * c[2][e] + weight[3] * c[3][e]
        )
        vote_ref[e] = top / bottom


def solution(mesh):
    n_rows = mesh.shape["rows"]
    in_specs = (
        P("rows", "cols"),
        P("pair", "rows", "cols"),
        P("pair", None, "rows", "cols"),
        P("pair"),
        P(),
        P(),
        P(),
        P(),
        P(),
        P(),
        P(),
    )
    out_specs = (P("pair", None, "rows", "cols"), P(None, "rows", "cols"))
    vmem = pl.BlockSpec(memory_space=pltpu.VMEM)
    hbm = pl.BlockSpec(memory_space=pltpu.HBM)
    dma = pltpu.SemaphoreType.DMA

    def shards(*args):
        args = [pltpu.with_memory_space_constraint(x, pltpu.HBM) for x in args]
        every = pl.pallas_call(
            functools.partial(kernel, n_rows),
            out_shape=pltpu.VMEM((4, 2, 8, 256), F32),
            in_specs=[hbm] * 11,
            out_specs=vmem,
            scratch_shapes=[
                pltpu.VMEM((8, 256), BF),
                pltpu.VMEM((2, 8, 256), BF),
                pltpu.SMEM((2,), jnp.int32),
                pltpu.VMEM((3, 128), BF),
                pltpu.VMEM((9, 2, 128), BF),
                pltpu.VMEM((128,), F32),
                pltpu.VMEM((2, 128), F32),
                pltpu.VMEM((9, 2, 128), BF),
                pltpu.SMEM((2,), F32),
                pltpu.VMEM((3, 32, RING), BF),
                pltpu.VMEM((32, 128), BF),
                pltpu.VMEM((2, 2, 24, RING), F32),
                pltpu.VMEM((2, 3, 2, 256, 256), BF),
                pltpu.VMEM((ROWS_X, RING), BF),
                pltpu.VMEM((ROWS_M, RING), BF),
                pltpu.VMEM((6, 32, 128), F32),
                pltpu.VMEM((128, 14 * 128), BF),
                pltpu.VMEM((6, 24, 128), F32),
                pltpu.VMEM((48, 5 * 256), BF),
                pltpu.VMEM((7, ROWS_X, 256), BF),
                pltpu.VMEM((6, ROWS_X, 256), BF),
                pltpu.VMEM((5, ROWS_X, 256), BF),
                pltpu.VMEM((3, 7 * Q, 256), F32),
                dma((9,)),
                dma((6,)),
                dma,
                dma((5,)),
                dma((5,)),
                dma((5,)),
                dma((5,)),
                dma((2,)),
                dma((2,)),
            ],
            compiler_params=pltpu.CompilerParams(
                collective_id=0, has_side_effects=True, vmem_limit_bytes=40 * 1024 * 1024
            ),
        )(*args)
        return pl.pallas_call(
            vote,
            out_shape=(
                jax.ShapeDtypeStruct((2, 2, 8, 256), F32),
                jax.ShapeDtypeStruct((2, 8, 256), F32),
            ),
            in_specs=[vmem],
            out_specs=(vmem, vmem),
        )(pltpu.with_memory_space_constraint(every, pltpu.VMEM))

    return jax.shard_map(shards, mesh=mesh, in_specs=in_specs, out_specs=out_specs, check_vma=False)
```

```python
import functools

import jax
import jax.numpy as jnp
from jax import lax
from jax.experimental import pallas as pl
from jax.experimental.pallas import tpu as pltpu
from jax.sharding import PartitionSpec as P

MESH = pl.DeviceIdType.MESH
BF = jnp.bfloat16
F32 = jnp.float32

sharpness = 4.0
max_shift = 2.0
OFF = -1e30

Q = 16
STRIDE = 17
ROWS_M = STRIDE * Q
ROWS_X = (STRIDE + 2) * Q
RING = 384


def dot(a, b, dims=((1,), (0,))):
    return lax.dot_general(a, b, (dims, ((), ())), preferred_element_type=F32)


def store_slabs(ref, index, y):
    ref[index, 0:ROWS_M, :] = y.astype(BF)
    first = pltpu.roll(y[0:Q], Q - 1, 0)
    second = pltpu.roll(y[Q : 2 * Q], Q - 1, 0)
    ref[index, ROWS_M:ROWS_X, :] = jnp.concatenate([first, second], axis=0).astype(BF)


def kernel(
    n_rows,
    src_in,
    tgt_in,
    prior_ref,
    off_in,
    table_in,
    inw_in,
    inb_in,
    hw_ref,
    hb_in,
    outw_in,
    outb_in,
    every,
    off_ref,
    table_ref,
    inw_ref,
    inb_ref,
    hb_ref,
    outw_ref,
    outb_ref,
    img,
    side,
    own_s,
    own_t,
    pri,
    wts,
    turned,
    order,
    gin,
    toe,
    gout,
    wout,
    feat,
    hid1,
    part1,
    part2,
    sums_out,
    part_of,
    bands,
    masks,
    in_sem,
    w_sem,
    p_sem,
    img_send,
    img_recv,
    pri_send,
    pri_recv,
    cand_send,
    cand_recv,
):
    pair = lax.axis_index("pair")
    row = lax.axis_index("rows")
    col = lax.axis_index("cols")
    has_up = row > 0
    has_down = row < n_rows - 1
    up = jnp.maximum(row - 1, 0)
    down = jnp.minimum(row + 1, n_rows - 1)
    other = 1 - col
    partner = 1 - pair
    tile_rows = 8
    rows_all = n_rows * tile_rows
    places = (
        (pair, up, col),
        (pair, down, col),
        (pair, row, other),
        (pair, up, other),
        (pair, down, other),
    )

    sends_to = (has_up, has_down, None, has_up, has_down)
    comes_from = (has_down, has_up, None, has_down, has_up)

    def only_if(condition, action):
        if condition is None:
            action()
        else:
            pl.when(condition)(action)

    def signal(place):
        pl.semaphore_signal(barrier, inc=1, device_id=place, device_id_type=MESH)

    barrier = pltpu.get_barrier_semaphore()
    for number in (0, 3, 1, 4, 2):
        only_if(sends_to[number], functools.partial(signal, places[number]))
    signal((partner, row, col))

    loads = []
    for number, (source, target) in enumerate(
        (
            (src_in, own_s),
            (tgt_in, own_t),
            (inw_in, inw_ref),
            (outw_in, outw_ref),
            (off_in, off_ref),
            (table_in, table_ref),
            (inb_in, inb_ref),
            (hb_in, hb_ref),
            (outb_in, outb_ref),
        )
    ):
        copy = pltpu.make_async_copy(source, target, in_sem.at[number])
        copy.start()
        loads.append(copy)

    weight_copies = []
    for number, (a, where, r0, l0) in enumerate(
        ((0, 0, 0, 0), (1, 0, 128, 0), (0, 0, 128, 128), (2, 1, 0, 0), (1, 1, 0, 128), (2, 1, 128, 128))
    ):
        copy = pltpu.make_async_copy(
            hw_ref.at[:, pl.ds(3 * a, 3)],
            wts.at[:, :, where, pl.ds(r0, 128), pl.ds(l0, 128)],
            w_sem.at[number],
        )
        copy.start()
        weight_copies.append(copy)
    own_prior = pltpu.make_async_copy(
        prior_ref, pri.at[:, :, pl.ds(8, 8), pl.ds(0, 256)], p_sem
    )
    own_prior.start()

    for copy in loads[:2]:
        copy.wait()
    own_rows = [own_s[...], own_t[0], own_t[1]]
    own = jnp.concatenate(
        [x.astype(F32) for x in own_rows] + [jnp.zeros((8, 256), F32)], axis=0
    ).astype(BF)
    img[0, :, 0:256] = own
    side[...] = jnp.where(col == 0, own[:, 128:256], own[:, 0:128])
    order[...] = jnp.zeros_like(order)

    m_slab = lax.broadcasted_iota(jnp.int32, (7, Q, 256), 0)
    m_chunk = lax.broadcasted_iota(jnp.int32, (7, Q, 256), 1)
    m_at = m_chunk * STRIDE + m_slab + col * 256
    for layer in range(3):
        inside = (m_at >= 3 - layer) & (m_at < 512 + 3 - layer)
        masks[layer] = jnp.where(inside, 1.0, 0.0).reshape(7 * Q, 256)

    for copy in loads[2:]:
        copy.wait()
    gin[...] = jnp.zeros_like(gin)
    for b in range(3):
        for ch in range(2):
            for a in range(3):
                w = inw_ref[3 * a + b, ch : ch + 1, :].astype(F32)
                gin[2 * b + ch, a : a + 1, :] = w
                gin[2 * b + ch, 16 + a : 17 + a, :] = w
    for r in range(14):
        start = (20 - r) % 16
        block = jnp.concatenate(
            [gin[g, start : start + 16, :] for g in range(6)] + [jnp.zeros((32, 128), F32)], axis=0
        )
        toe[:, r * 128 : (r + 1) * 128] = block.astype(BF)

    gout[...] = jnp.zeros_like(gout)
    for b in range(3):
        for e in range(2):
            for a in range(3):
                gout[2 * b + e, 10 - a : 11 - a, :] = outw_ref[3 * a + b, e : e + 1, :].astype(F32)
    for p in range(5):
        for h in range(2):
            start = 10 - (2 * p + h)
            block = jnp.concatenate(
                [gout[g, start : start + 8, :] for g in range(6)] + [jnp.zeros((80, 128), F32)], axis=0
            )
            wout[p, h * 128 : (h + 1) * 128, :] = jnp.transpose(block).astype(BF)

    for layer in range(2):
        for b in range(3):
            wts[layer, b, 0, 0:128, 128:256] = jnp.zeros((128, 128), BF)
            wts[layer, b, 1, 128:256, 0:128] = jnp.zeros((128, 128), BF)

    pl.semaphore_wait(barrier, 2 + 2 * has_up.astype(jnp.int32) + 2 * has_down.astype(jnp.int32))

    main = pl.ds(0, 256)
    edge = pl.ds(256, 128)
    half = pl.ds(pl.multiple_of((1 - col) * 128, 128), 128)
    routes = ((2, main), (1, main), (0, edge), (2, edge), (1, edge))
    image_copies = [None] * 5
    for number in (0, 3, 1, 4, 2):
        slot, lanes = routes[number]
        copy = pltpu.make_async_remote_copy(
            src_ref=img.at[0, :, main] if number < 2 else side,
            dst_ref=img.at[slot, :, lanes],
            send_sem=img_send.at[number],
            recv_sem=img_recv.at[number],
            device_id=places[number],
            device_id_type=MESH,
        )
        only_if(sends_to[number], copy.start)
        image_copies[number] = copy
    prior_copies = []
    for number, (slot, lanes) in enumerate(routes):
        start = (8, 0, 16)[slot]
        copy = pltpu.make_async_remote_copy(
            src_ref=prior_ref if number < 2 else prior_ref.at[:, :, :, half],
            dst_ref=pri.at[:, :, pl.ds(start, 8), lanes],
            send_sem=pri_send.at[number],
            recv_sem=pri_recv.at[number],
            device_id=places[number],
            device_id_type=MESH,
        )
        only_if(sends_to[number], copy.start)
        prior_copies.append(copy)

    lane8 = lax.broadcasted_iota(jnp.int32, (8, RING), 1)
    sub8 = lax.broadcasted_iota(jnp.int32, (8, RING), 0)
    lanes_ok = (lane8 < 256) | ((lane8 < 320) == (col == 0))
    above_ok = jnp.logical_and(lanes_ok, has_up)
    below_ok = jnp.logical_and(lanes_ok, has_down)
    blank = jnp.zeros((8, RING), F32)

    def gather_columns(rows_of):
        three = [rows_of(s) for s in range(3)]
        space = [blank] * 4
        stack = jnp.concatenate(
            list(three[0] + three[1]) + space + list(three[0] + three[2]) + space, axis=0
        )
        turned[4 : RING + 4, :] = jnp.transpose(stack)
        turned[0:4, :] = turned[RING : RING + 4, :]
        slabs = [turned[pl.ds(i, Q, STRIDE), :] for i in range(STRIDE + 2)]
        group = lax.broadcasted_iota(jnp.int32, (ROWS_M, 128), 1) // 32
        out = []
        for k in range(2):
            moved = [
                jnp.concatenate(slabs[b : b + STRIDE], axis=0)
                if (32 * b - 64 * k) % 128 == 0
                else pltpu.roll(jnp.concatenate(slabs[b : b + STRIDE], axis=0), (32 * b - 64 * k) % 128, 1)
                for b in range(3)
            ]
            out.append(
                jnp.where(group == 0, moved[0], jnp.where(group == 1, moved[1], moved[2])).astype(BF)
            )
        return out

    def image(slot, s):
        return img[slot].astype(F32)[8 * s : 8 * s + 8]

    def own_image(s):
        return (jnp.where(lanes_ok, image(0, s), 0.0), blank)

    def halo_rows(s):
        above = jnp.where(above_ok, image(1, s), 0.0)
        below = jnp.where(below_ok, image(2, s), 0.0)
        return (blank, jnp.where(sub8 < 4, below, above))

    def row_bias(bias, first_row):
        which = first_row + lax.broadcasted_iota(jnp.int32, (1, 256), 1) // 128
        return jnp.where((which >= 0) & (which < rows_all), bias, OFF)

    def twice(vector):
        return jnp.concatenate([vector, vector], axis=1)

    def finish(total, bias, layer):
        y = jnp.maximum(total + bias, 0.0)
        return jnp.concatenate([y[0 : 7 * Q] * masks[layer], y[7 * Q :]], axis=0)

    def first_layer(k, p, lhs):
        total = dot(lhs, toe[:, p * 256 : (p + 1) * 256])
        bias_here = row_bias(first_bias[k], row * tile_rows + 2 * p - 3)
        store_slabs(feat.at[k], p, finish(total, bias_here, 0))

    def taps(source, k, p, layer, wheres):
        total = None
        for where in wheres:
            for b in range(3):
                term = dot(source[k, p + where, b * Q : b * Q + ROWS_M, :], wts[layer, b, where])
                total = term if total is None else total + term
        return total

    hidden_layers = ((feat, part1), (hid1, part2))

    def hidden(k, p, layer, wheres=(0, 1), part=None):
        source, sums = hidden_layers[layer]
        total = taps(source, k, p, layer, wheres)
        if part is not None:
            total = total + sums[k, part]
        bias_here = row_bias(hidden_bias[layer], row * tile_rows + 2 * p - 2 + layer)
        y = finish(total, bias_here, layer + 1)
        if layer == 0:
            store_slabs(hid1.at[k], p, y)
            return None
        part_of[k, p] = y.astype(BF)
        return None

    def partial(k, p, layer, where, part):
        source, sums = hidden_layers[layer]
        sums[k, part] = taps(source, k, p, layer, (where,))

    table = table_ref[...].astype(F32)
    in_bias = inb_ref[...].reshape(1, 128)
    hidden_bias = [twice(hb_ref[layer : layer + 1, :]) for layer in range(2)]
    first_bias = []
    for k in range(2):
        embed = jnp.zeros((1, 128), F32)
        for o in range(table.shape[0]):
            embed = embed + jnp.where(off_ref[k] == o, table[o : o + 1], 0.0)
        first_bias.append(twice(in_bias + embed))

    image_copies[2].wait_recv()
    lhs_own = gather_columns(own_image)
    for k in range(2):
        for p in (2, 3, 4):
            first_layer(k, p, lhs_own[k])
    for copy in weight_copies:
        copy.wait()
    for k in range(2):
        for p in (2, 3):
            hidden(k, p, 0)
    for k in range(2):
        partial(k, 1, 0, 1, 0)
        partial(k, 4, 0, 0, 1)
    for k in range(2):
        hidden(k, 2, 1)
    for k in range(2):
        partial(k, 1, 1, 1, 0)
        partial(k, 3, 1, 0, 1)
    for k in range(2):
        sums_out[k] = dot(part_of[k, 2], wout[2])

    for number in (0, 1, 3, 4):
        only_if(comes_from[number], image_copies[number].wait_recv)
    lhs = [a + b for a, b in zip(lhs_own, gather_columns(halo_rows))]
    for k in range(2):
        for p in (0, 1, 5, 6):
            first_layer(k, p, lhs[k])
    for k in range(2):
        hidden(k, 0, 0)
        hidden(k, 1, 0, (0,), 0)
        hidden(k, 4, 0, (1,), 1)
        hidden(k, 5, 0)
    for number in range(5):
        only_if(comes_from[number], prior_copies[number].wait_recv)
    own_prior.wait()
    for k in range(2):
        hidden(k, 0, 1)
        hidden(k, 1, 1, (0,), 0)
        hidden(k, 3, 1, (1,), 1)
        hidden(k, 4, 1)
    flat = []
    for k in range(2):
        total = sums_out[k]
        for p in (0, 1, 3, 4):
            total = total + dot(part_of[k, p], wout[p])
        flat.append(total)
    for k in range(2):
        for e in range(2):
            pri[k, e, 0:8, :] = jnp.where(above_ok, pri[k, e, 0:8, :], 0.0)
            pri[k, e, 8:16, :] = jnp.where(lanes_ok, pri[k, e, 8:16, :], 0.0)
            pri[k, e, 16:24, :] = jnp.where(below_ok, pri[k, e, 16:24, :], 0.0)
            for rs in range(5):
                band = pri[k, e, 6 + rs : 14 + rs, :]
                for cs in range(5):
                    moved = band if cs == 2 else pltpu.roll(band, (RING + 2 - cs) % RING, 1)
                    bands[k, e, rs, cs] = moved[:, 0:256]

    for k in range(2):
        for i in range(STRIDE):
            order[k, pl.ds(i, Q, STRIDE), :] = flat[k][i * Q : (i + 1) * Q]
        natural = jnp.transpose(order[k])
        flow = []
        for e in range(2):
            z0 = natural[8 * e : 8 * e + 8]
            z1 = pltpu.roll(natural[16 + 8 * e : 24 + 8 * e], RING - 1, 1)
            z2 = pltpu.roll(natural[32 + 8 * e : 40 + 8 * e], RING - 2, 1)
            flow.append(max_shift * jnp.tanh((z0 + z1 + z2)[:, 0:256] + outb_ref[e]))
        row_weight = [jnp.maximum(1.0 - jnp.abs(flow[0] - s), 0.0) for s in range(-2, 3)]
        col_weight = [jnp.maximum(1.0 - jnp.abs(flow[1] - s), 0.0) for s in range(-2, 3)]
        mine = pair * 2 + k
        for e in range(2):
            value = flow[e]
            for rs in range(5):
                inner = None
                for cs in range(5):
                    term = col_weight[cs] * bands[k, e, rs, cs]
                    inner = term if inner is None else inner + term
                value = value + row_weight[rs] * inner
            every[mine, e] = value
        copy = pltpu.make_async_remote_copy(
            src_ref=every.at[mine],
            dst_ref=every.at[mine],
            send_sem=cand_send.at[k],
            recv_sem=cand_recv.at[k],
            device_id=(partner, row, col),
            device_id_type=MESH,
        )
        copy.start()
        if k == 0:
            first_copy = copy
        else:
            second_copy = copy

    first_copy.wait()
    second_copy.wait()
    for number in range(5):
        only_if(sends_to[number], image_copies[number].wait_send)
        only_if(sends_to[number], prior_copies[number].wait_send)


def vote(every, cand_ref, vote_ref):
    pair = lax.axis_index("pair")
    for k in range(2):
        cand_ref[k] = every[2 * pair + k]
    c = [[every[k, e] for e in range(2)] for k in range(4)]
    score = [None] * 4
    for i in range(4):
        for j in range(i + 1, 4):
            dr = c[i][0] - c[j][0]
            dc = c[i][1] - c[j][1]
            apart = dr * dr + dc * dc
            score[i] = apart if score[i] is None else score[i] + apart
            score[j] = apart if score[j] is None else score[j] + apart
    weight = [jnp.exp(score[i] * (-1.0 / (3 * sharpness))) for i in range(4)]
    bottom = (weight[0] + weight[1]) + (weight[2] + weight[3])
    for e in range(2):
        top = (weight[0] * c[0][e] + weight[1] * c[1][e]) + (
            weight[2] * c[2][e] + weight[3] * c[3][e]
        )
        vote_ref[e] = top / bottom


def solution(mesh):
    n_rows = mesh.shape["rows"]
    in_specs = (
        P("rows", "cols"),
        P("pair", "rows", "cols"),
        P("pair", None, "rows", "cols"),
        P("pair"),
        P(),
        P(),
        P(),
        P(),
        P(),
        P(),
        P(),
    )
    out_specs = (P("pair", None, "rows", "cols"), P(None, "rows", "cols"))
    vmem = pl.BlockSpec(memory_space=pltpu.VMEM)
    hbm = pl.BlockSpec(memory_space=pltpu.HBM)
    dma = pltpu.SemaphoreType.DMA

    def shards(*args):
        args = [pltpu.with_memory_space_constraint(x, pltpu.HBM) for x in args]
        every = pl.pallas_call(
            functools.partial(kernel, n_rows),
            out_shape=pltpu.VMEM((4, 2, 8, 256), F32),
            in_specs=[hbm] * 11,
            out_specs=vmem,
            scratch_shapes=[
                pltpu.SMEM((2,), jnp.int32),
                pltpu.VMEM((3, 128), BF),
                pltpu.VMEM((9, 2, 128), BF),
                pltpu.VMEM((128,), F32),
                pltpu.VMEM((2, 128), F32),
                pltpu.VMEM((9, 2, 128), BF),
                pltpu.SMEM((2,), F32),
                pltpu.VMEM((3, 32, RING), BF),
                pltpu.VMEM((32, 128), BF),
                pltpu.VMEM((8, 256), BF),
                pltpu.VMEM((2, 8, 256), BF),
                pltpu.VMEM((2, 2, 24, RING), F32),
                pltpu.VMEM((2, 3, 2, 256, 256), BF),
                pltpu.VMEM((RING + 8, 128), F32),
                pltpu.VMEM((2, RING, 128), F32),
                pltpu.VMEM((6, 32, 128), F32),
                pltpu.VMEM((128, 14 * 128), BF),
                pltpu.VMEM((6, 24, 128), F32),
                pltpu.VMEM((5, 256, 128), BF),
                pltpu.VMEM((2, 7, ROWS_X, 256), BF),
                pltpu.VMEM((2, 6, ROWS_X, 256), BF),
                pltpu.VMEM((2, 2, ROWS_M, 256), F32),
                pltpu.VMEM((2, 2, ROWS_M, 256), F32),
                pltpu.VMEM((2, ROWS_M, 128), F32),
                pltpu.VMEM((2, 5, ROWS_M, 256), BF),
                pltpu.VMEM((2, 2, 5, 5, 8, 256), F32),
                pltpu.VMEM((3, 7 * Q, 256), F32),
                dma((9,)),
                dma((6,)),
                dma,
                dma((5,)),
                dma((5,)),
                dma((5,)),
                dma((5,)),
                dma((2,)),
                dma((2,)),
            ],
            compiler_params=pltpu.CompilerParams(
                collective_id=0, has_side_effects=True, vmem_limit_bytes=40 * 1024 * 1024
            ),
        )(*args)
        return pl.pallas_call(
            vote,
            out_shape=(
                jax.ShapeDtypeStruct((2, 2, 8, 256), F32),
                jax.ShapeDtypeStruct((2, 8, 256), F32),
            ),
            in_specs=[vmem],
            out_specs=(vmem, vmem),
        )(pltpu.with_memory_space_constraint(every, pltpu.VMEM))

    return jax.shard_map(shards, mesh=mesh, in_specs=in_specs, out_specs=out_specs, check_vma=False)
```

```python
import functools

import jax
import jax.numpy as jnp
from jax import lax
from jax.experimental import pallas as pl
from jax.experimental.pallas import tpu as pltpu
from jax.sharding import PartitionSpec as P

MESH = pl.DeviceIdType.MESH
BF = jnp.bfloat16
F32 = jnp.float32

sharpness = 4.0
max_shift = 2.0
OFF = -1e30

Q = 16
STRIDE = 17
ROWS_M = STRIDE * Q
ROWS_X = (STRIDE + 2) * Q
RING = 384


def dot(a, b, dims=((1,), (0,))):
    return lax.dot_general(a, b, (dims, ((), ())), preferred_element_type=F32)


def store_slabs(ref, index, y, low=0):
    ref[index, low : low + y.shape[0], :] = y.astype(BF)
    if low == 0:
        first = pltpu.roll(y[0:Q], Q - 1, 0)
        second = pltpu.roll(y[Q : 2 * Q], Q - 1, 0)
        ref[index, ROWS_M:ROWS_X, :] = jnp.concatenate([first, second], axis=0).astype(BF)


def kernel(
    n_rows,
    src_in,
    tgt_in,
    prior_ref,
    off_in,
    table_in,
    inw_in,
    inb_in,
    hw_ref,
    hb_in,
    outw_in,
    outb_in,
    every,
    off_ref,
    table_ref,
    inw_ref,
    inb_ref,
    hb_ref,
    outw_ref,
    outb_ref,
    img,
    side,
    own_s,
    own_t,
    pri,
    wts,
    turned,
    order,
    gin,
    toe,
    gout,
    wout,
    feat,
    hid1,
    part1,
    part2,
    sums_out,
    own_lhs,
    part_of,
    bands,
    masks,
    in_sem,
    w_sem,
    p_sem,
    img_send,
    img_recv,
    pri_send,
    pri_recv,
    cand_send,
    cand_recv,
):
    pair = lax.axis_index("pair")
    row = lax.axis_index("rows")
    col = lax.axis_index("cols")
    has_up = row > 0
    has_down = row < n_rows - 1
    up = jnp.maximum(row - 1, 0)
    down = jnp.minimum(row + 1, n_rows - 1)
    other = 1 - col
    partner = 1 - pair
    tile_rows = 8
    rows_all = n_rows * tile_rows
    places = (
        (pair, up, col),
        (pair, down, col),
        (pair, row, other),
        (pair, up, other),
        (pair, down, other),
    )

    sends_to = (has_up, has_down, None, has_up, has_down)
    comes_from = (has_down, has_up, None, has_down, has_up)

    def only_if(condition, action):
        if condition is None:
            action()
        else:
            pl.when(condition)(action)

    def signal(place):
        pl.semaphore_signal(barrier, inc=1, device_id=place, device_id_type=MESH)

    barrier = pltpu.get_barrier_semaphore()
    for number in (0, 3, 1, 4, 2):
        only_if(sends_to[number], functools.partial(signal, places[number]))
    signal((partner, row, col))

    loads = []
    for number, (source, target) in enumerate(
        (
            (src_in, own_s),
            (tgt_in, own_t),
            (inw_in, inw_ref),
            (outw_in, outw_ref),
            (off_in, off_ref),
            (table_in, table_ref),
            (inb_in, inb_ref),
            (hb_in, hb_ref),
            (outb_in, outb_ref),
        )
    ):
        copy = pltpu.make_async_copy(source, target, in_sem.at[number])
        copy.start()
        loads.append(copy)

    weight_copies = []
    for number, (a, where, r0, l0) in enumerate(
        ((0, 0, 0, 0), (1, 0, 128, 0), (0, 0, 128, 128), (2, 1, 0, 0), (1, 1, 0, 128), (2, 1, 128, 128))
    ):
        copy = pltpu.make_async_copy(
            hw_ref.at[:, pl.ds(3 * a, 3)],
            wts.at[:, :, where, pl.ds(r0, 128), pl.ds(l0, 128)],
            w_sem.at[number],
        )
        copy.start()
        weight_copies.append(copy)
    own_prior = pltpu.make_async_copy(
        prior_ref, pri.at[:, :, pl.ds(8, 8), pl.ds(0, 256)], p_sem
    )
    own_prior.start()

    for copy in loads[:2]:
        copy.wait()
    own_rows = [own_s[...], own_t[0], own_t[1]]
    own = jnp.concatenate(
        [x.astype(F32) for x in own_rows] + [jnp.zeros((8, 256), F32)], axis=0
    ).astype(BF)
    img[0, :, 0:256] = own
    side[...] = jnp.where(col == 0, own[:, 128:256], own[:, 0:128])
    for copy in loads[2:]:
        copy.wait()

    lane8 = lax.broadcasted_iota(jnp.int32, (8, RING), 1)
    sub8 = lax.broadcasted_iota(jnp.int32, (8, RING), 0)
    lanes_ok = (lane8 < 256) | ((lane8 < 320) == (col == 0))
    above_ok = jnp.logical_and(lanes_ok, has_up)
    below_ok = jnp.logical_and(lanes_ok, has_down)
    blank = jnp.zeros((8, RING), F32)

    def gather_columns(rows_of):
        three = [rows_of(s) for s in range(3)]
        space = [blank] * 4
        stack = jnp.concatenate(
            list(three[0] + three[1]) + space + list(three[0] + three[2]) + space, axis=0
        )
        turned[4 : RING + 4, :] = jnp.transpose(stack)
        turned[0:4, :] = turned[RING : RING + 4, :]
        slabs = [turned[pl.ds(i, Q, STRIDE), :] for i in range(STRIDE + 2)]
        group = lax.broadcasted_iota(jnp.int32, (ROWS_M, 128), 1) // 32
        out = []
        for k in range(2):
            moved = [
                jnp.concatenate(slabs[b : b + STRIDE], axis=0)
                if (32 * b - 64 * k) % 128 == 0
                else pltpu.roll(jnp.concatenate(slabs[b : b + STRIDE], axis=0), (32 * b - 64 * k) % 128, 1)
                for b in range(3)
            ]
            out.append(
                jnp.where(group == 0, moved[0], jnp.where(group == 1, moved[1], moved[2])).astype(BF)
            )
        return out

    def image(slot, s):
        return img[slot].astype(F32)[8 * s : 8 * s + 8]

    def own_image(s):
        return (jnp.where(lanes_ok, image(0, s), 0.0), blank)

    def own_image_alone(s):
        mine = img[0, :, 0:256].astype(F32)[8 * s : 8 * s + 8]
        return (jnp.concatenate([mine, jnp.zeros((8, 128), F32)], axis=1), blank)

    def above_rows(s):
        return (blank, jnp.where(jnp.logical_and(sub8 >= 4, above_ok), image(1, s), 0.0))

    def below_rows(s):
        return (blank, jnp.where(jnp.logical_and(sub8 < 4, below_ok), image(2, s), 0.0))

    def halo_rows(s):
        return (blank, jnp.where(sub8 < 4, below_rows(s)[1], above_rows(s)[1]))

    def row_bias(bias, first_row):
        which = first_row + lax.broadcasted_iota(jnp.int32, (1, 256), 1) // 128
        return jnp.where((which >= 0) & (which < rows_all), bias, OFF)

    def twice(vector):
        return jnp.concatenate([vector, vector], axis=1)

    def finish(total, bias, layer, low=0):
        y = jnp.maximum(total + bias, 0.0)
        if low > 0:
            return y
        count = min(7 * Q, y.shape[0])
        masked = y[0:count] * masks[layer, 0:count, :]
        return masked if count == y.shape[0] else jnp.concatenate([masked, y[count:]], axis=0)

    def first_layer(k, p, lhs):
        total = dot(lhs, toe[:, p * 256 : (p + 1) * 256])
        bias_here = row_bias(first_bias[k], row * tile_rows + 2 * p - 3)
        store_slabs(feat.at[k], p, finish(total, bias_here, 0))

    def taps(source, k, p, layer, wheres, low, count):
        total = None
        for where in wheres:
            for b in range(3):
                rows = source[k, p + where, b * Q + low : b * Q + low + count, :]
                term = dot(rows, wts[layer, b, where])
                total = term if total is None else total + term
        return total

    hidden_layers = ((feat, part1), (hid1, part2))

    def hidden(k, p, layer, wheres=(0, 1), part=None, low=0, count=ROWS_M):
        source, sums = hidden_layers[layer]
        total = taps(source, k, p, layer, wheres, low, count)
        if part is not None:
            total = total + sums[k, part]
        bias_here = row_bias(hidden_bias[layer], row * tile_rows + 2 * p - 2 + layer)
        y = finish(total, bias_here, layer + 1, low)
        if layer == 0:
            store_slabs(hid1.at[k], p, y, low)
        else:
            part_of[k, p, low : low + count, :] = y.astype(BF)

    def partial(k, p, layer, where, part, low=0, count=ROWS_M):
        source, sums = hidden_layers[layer]
        sums[k, part, low : low + count, :] = taps(source, k, p, layer, (where,), low, count)

    table = table_ref[...].astype(F32)
    in_bias = inb_ref[...].reshape(1, 128)
    hidden_bias = [twice(hb_ref[layer : layer + 1, :]) for layer in range(2)]
    first_bias = []
    for k in range(2):
        embed = jnp.zeros((1, 128), F32)
        for o in range(table.shape[0]):
            embed = embed + jnp.where(off_ref[k] == o, table[o : o + 1], 0.0)
        first_bias.append(twice(in_bias + embed))

    main = pl.ds(0, 256)
    edge = pl.ds(256, 128)
    half = pl.ds(pl.multiple_of((1 - col) * 128, 128), 128)
    routes = ((2, main), (1, main), (0, edge), (2, edge), (1, edge))
    prior_copies = []
    for number, (slot, lanes) in enumerate(routes):
        start = (8, 0, 16)[slot]
        copy = pltpu.make_async_remote_copy(
            src_ref=prior_ref if number < 2 else prior_ref.at[:, :, :, half],
            dst_ref=pri.at[:, :, pl.ds(start, 8), lanes],
            send_sem=pri_send.at[number],
            recv_sem=pri_recv.at[number],
            device_id=places[number],
            device_id_type=MESH,
        )
        prior_copies.append(copy)

    def send_priors():
        for number in range(5):
            only_if(sends_to[number], prior_copies[number].start)

    def make_constants():
        order[...] = jnp.zeros_like(order)

        m_slab = lax.broadcasted_iota(jnp.int32, (7, Q, 256), 0)
        m_chunk = lax.broadcasted_iota(jnp.int32, (7, Q, 256), 1)
        m_at = m_chunk * STRIDE + m_slab + col * 256
        for layer in range(3):
            inside = (m_at >= 3 - layer) & (m_at < 512 + 3 - layer)
            masks[layer] = jnp.where(inside, 1.0, 0.0).reshape(7 * Q, 256)

        gin[...] = jnp.zeros_like(gin)
        for b in range(3):
            for ch in range(2):
                for a in range(3):
                    w = inw_ref[3 * a + b, ch : ch + 1, :].astype(F32)
                    gin[2 * b + ch, a : a + 1, :] = w
                    gin[2 * b + ch, 16 + a : 17 + a, :] = w
        for r in range(14):
            start = (20 - r) % 16
            block = jnp.concatenate(
                [gin[g, start : start + 16, :] for g in range(6)] + [jnp.zeros((32, 128), F32)], axis=0
            )
            toe[:, r * 128 : (r + 1) * 128] = block.astype(BF)

        gout[...] = jnp.zeros_like(gout)
        for b in range(3):
            for e in range(2):
                for a in range(3):
                    gout[2 * b + e, 10 - a : 11 - a, :] = outw_ref[3 * a + b, e : e + 1, :].astype(F32)
        for p in range(5):
            for h in range(2):
                start = 10 - (2 * p + h)
                block = jnp.concatenate(
                    [gout[g, start : start + 8, :] for g in range(6)] + [jnp.zeros((80, 128), F32)], axis=0
                )
                wout[p, h * 128 : (h + 1) * 128, :] = jnp.transpose(block).astype(BF)

        for layer in range(2):
            for b in range(3):
                wts[layer, b, 0, 0:128, 128:256] = jnp.zeros((128, 128), BF)
                wts[layer, b, 1, 128:256, 0:128] = jnp.zeros((128, 128), BF)


    def own_first(rows_of):
        columns = gather_columns(rows_of)
        for k in range(2):
            own_lhs[k] = columns[k]
            for p in (2, 3, 4):
                first_layer(k, p, columns[k])

    def own_hidden(first_ranges, second_ranges):
        for low, count in first_ranges:
            for k in range(2):
                for p in (2, 3):
                    hidden(k, p, 0, low=low, count=count)
            for k in range(2):
                partial(k, 1, 0, 1, 0, low, count)
                partial(k, 4, 0, 0, 1, low, count)
        for low, count in second_ranges:
            for k in range(2):
                hidden(k, 2, 1, low=low, count=count)
            for k in range(2):
                partial(k, 1, 1, 1, 0, low, count)
                partial(k, 3, 1, 0, 1, low, count)
        for low, count in second_ranges:
            for k in range(2):
                sums_out[k, low : low + count, :] = dot(part_of[k, 2, low : low + count, :], wout[2])

    def wait_weights():
        for copy in weight_copies:
            copy.wait()

    whole = ((0, ROWS_M),)
    early = jnp.logical_and(row % 8 == 0, jnp.logical_and(row != 0, row != n_rows // 2))

    @pl.when(early)
    def _():
        make_constants()
        own_first(own_image_alone)
        wait_weights()
        own_hidden(whole, whole)

    pl.semaphore_wait(barrier, 2 + 2 * has_up.astype(jnp.int32) + 2 * has_down.astype(jnp.int32))

    image_copies = [None] * 5
    for number in (2, 0, 3, 1, 4):
        slot, lanes = routes[number]
        copy = pltpu.make_async_remote_copy(
            src_ref=img.at[0, :, main] if number < 2 else side,
            dst_ref=img.at[slot, :, lanes],
            send_sem=img_send.at[number],
            recv_sem=img_recv.at[number],
            device_id=places[number],
            device_id_type=MESH,
        )
        only_if(sends_to[number], copy.start)
        image_copies[number] = copy

    @pl.when(early)
    def _():
        send_priors()
        image_copies[2].wait_recv()
        own_first(own_image)
        own_hidden(((0, 5 * Q),), ((0, 4 * Q), (16 * Q, Q)))

    @pl.when(jnp.logical_not(early))
    def _():
        make_constants()
        image_copies[2].wait_recv()
        own_first(own_image)
        send_priors()
        wait_weights()
        own_hidden(whole, whole)

    def outer(rows_of, sides, arrivals):
        for number in arrivals:
            only_if(comes_from[number], image_copies[number].wait_recv)
        more = gather_columns(rows_of)
        for k in range(2):
            lhs = own_lhs[k] + more[k]
            for side_of in sides:
                for p in ((0, 1), (5, 6))[side_of]:
                    first_layer(k, p, lhs)
        for k in range(2):
            for side_of in sides:
                hidden(k, (0, 5)[side_of], 0)
                hidden(k, (1, 4)[side_of], 0, (side_of,), side_of)
        for k in range(2):
            for side_of in sides:
                hidden(k, (0, 4)[side_of], 1)
                hidden(k, (1, 3)[side_of], 1, (side_of,), side_of)
        for k in range(2):
            total = sums_out[k]
            for side_of in sides:
                for p in ((0, 1), (4, 3))[side_of]:
                    total = total + dot(part_of[k, p], wout[p])
            sums_out[k] = total

    middle = n_rows // 2
    below_first = jnp.logical_or(row == middle, jnp.logical_and(row % 8 == 1, row > 1))
    above_first = row == middle - 1

    @pl.when(below_first)
    def _():
        outer(below_rows, (1,), (0, 3))
        outer(above_rows, (0,), (1, 4))

    @pl.when(above_first)
    def _():
        outer(above_rows, (0,), (1, 4))
        outer(below_rows, (1,), (0, 3))

    @pl.when(jnp.logical_not(jnp.logical_or(below_first, above_first)))
    def _():
        outer(halo_rows, (0, 1), (0, 1, 3, 4))

    for number in range(5):
        only_if(comes_from[number], prior_copies[number].wait_recv)
    own_prior.wait()
    for k in range(2):
        for e in range(2):
            pri[k, e, 0:8, :] = jnp.where(above_ok, pri[k, e, 0:8, :], 0.0)
            pri[k, e, 8:16, :] = jnp.where(lanes_ok, pri[k, e, 8:16, :], 0.0)
            pri[k, e, 16:24, :] = jnp.where(below_ok, pri[k, e, 16:24, :], 0.0)
            for rs in range(5):
                band = pri[k, e, 6 + rs : 14 + rs, :]
                for cs in range(5):
                    moved = band if cs == 2 else pltpu.roll(band, (RING + 2 - cs) % RING, 1)
                    bands[k, e, rs, cs] = moved[:, 0:256]

    for k in range(2):
        for i in range(STRIDE):
            order[k, pl.ds(i, Q, STRIDE), :] = sums_out[k, i * Q : (i + 1) * Q, :]
        natural = jnp.transpose(order[k])
        flow = []
        for e in range(2):
            z0 = natural[8 * e : 8 * e + 8]
            z1 = pltpu.roll(natural[16 + 8 * e : 24 + 8 * e], RING - 1, 1)
            z2 = pltpu.roll(natural[32 + 8 * e : 40 + 8 * e], RING - 2, 1)
            flow.append(max_shift * jnp.tanh((z0 + z1 + z2)[:, 0:256] + outb_ref[e]))
        row_weight = [jnp.maximum(1.0 - jnp.abs(flow[0] - s), 0.0) for s in range(-2, 3)]
        col_weight = [jnp.maximum(1.0 - jnp.abs(flow[1] - s), 0.0) for s in range(-2, 3)]
        mine = pair * 2 + k
        for e in range(2):
            value = flow[e]
            for rs in range(5):
                inner = None
                for cs in range(5):
                    term = col_weight[cs] * bands[k, e, rs, cs]
                    inner = term if inner is None else inner + term
                value = value + row_weight[rs] * inner
            every[mine, e] = value
        copy = pltpu.make_async_remote_copy(
            src_ref=every.at[mine],
            dst_ref=every.at[mine],
            send_sem=cand_send.at[k],
            recv_sem=cand_recv.at[k],
            device_id=(partner, row, col),
            device_id_type=MESH,
        )
        copy.start()
        if k == 0:
            first_copy = copy
        else:
            second_copy = copy

    first_copy.wait()
    second_copy.wait()
    for number in range(5):
        only_if(sends_to[number], image_copies[number].wait_send)
        only_if(sends_to[number], prior_copies[number].wait_send)


def vote(every, cand_ref, vote_ref):
    pair = lax.axis_index("pair")
    for k in range(2):
        cand_ref[k] = every[2 * pair + k]
    c = [[every[k, e] for e in range(2)] for k in range(4)]
    score = [None] * 4
    for i in range(4):
        for j in range(i + 1, 4):
            dr = c[i][0] - c[j][0]
            dc = c[i][1] - c[j][1]
            apart = dr * dr + dc * dc
            score[i] = apart if score[i] is None else score[i] + apart
            score[j] = apart if score[j] is None else score[j] + apart
    weight = [jnp.exp(score[i] * (-1.0 / (3 * sharpness))) for i in range(4)]
    bottom = (weight[0] + weight[1]) + (weight[2] + weight[3])
    for e in range(2):
        top = (weight[0] * c[0][e] + weight[1] * c[1][e]) + (
            weight[2] * c[2][e] + weight[3] * c[3][e]
        )
        vote_ref[e] = top / bottom


def solution(mesh):
    n_rows = mesh.shape["rows"]
    in_specs = (
        P("rows", "cols"),
        P("pair", "rows", "cols"),
        P("pair", None, "rows", "cols"),
        P("pair"),
        P(),
        P(),
        P(),
        P(),
        P(),
        P(),
        P(),
    )
    out_specs = (P("pair", None, "rows", "cols"), P(None, "rows", "cols"))
    vmem = pl.BlockSpec(memory_space=pltpu.VMEM)
    hbm = pl.BlockSpec(memory_space=pltpu.HBM)
    dma = pltpu.SemaphoreType.DMA

    def shards(*args):
        args = [pltpu.with_memory_space_constraint(x, pltpu.HBM) for x in args]
        every = pl.pallas_call(
            functools.partial(kernel, n_rows),
            out_shape=pltpu.VMEM((4, 2, 8, 256), F32),
            in_specs=[hbm] * 11,
            out_specs=vmem,
            scratch_shapes=[
                pltpu.SMEM((2,), jnp.int32),
                pltpu.VMEM((3, 128), BF),
                pltpu.VMEM((9, 2, 128), BF),
                pltpu.VMEM((128,), F32),
                pltpu.VMEM((2, 128), F32),
                pltpu.VMEM((9, 2, 128), BF),
                pltpu.SMEM((2,), F32),
                pltpu.VMEM((3, 32, RING), BF),
                pltpu.VMEM((32, 128), BF),
                pltpu.VMEM((8, 256), BF),
                pltpu.VMEM((2, 8, 256), BF),
                pltpu.VMEM((2, 2, 24, RING), F32),
                pltpu.VMEM((2, 3, 2, 256, 256), BF),
                pltpu.VMEM((RING + 8, 128), F32),
                pltpu.VMEM((2, RING, 128), F32),
                pltpu.VMEM((6, 32, 128), F32),
                pltpu.VMEM((128, 14 * 128), BF),
                pltpu.VMEM((6, 24, 128), F32),
                pltpu.VMEM((5, 256, 128), BF),
                pltpu.VMEM((2, 7, ROWS_X, 256), BF),
                pltpu.VMEM((2, 6, ROWS_X, 256), BF),
                pltpu.VMEM((2, 2, ROWS_M, 256), F32),
                pltpu.VMEM((2, 2, ROWS_M, 256), F32),
                pltpu.VMEM((2, ROWS_M, 128), F32),
                pltpu.VMEM((2, ROWS_M, 128), BF),
                pltpu.VMEM((2, 5, ROWS_M, 256), BF),
                pltpu.VMEM((2, 2, 5, 5, 8, 256), F32),
                pltpu.VMEM((3, 7 * Q, 256), F32),
                dma((9,)),
                dma((6,)),
                dma,
                dma((5,)),
                dma((5,)),
                dma((5,)),
                dma((5,)),
                dma((2,)),
                dma((2,)),
            ],
            compiler_params=pltpu.CompilerParams(
                collective_id=0, has_side_effects=True, vmem_limit_bytes=40 * 1024 * 1024
            ),
        )(*args)
        return pl.pallas_call(
            vote,
            out_shape=(
                jax.ShapeDtypeStruct((2, 2, 8, 256), F32),
                jax.ShapeDtypeStruct((2, 8, 256), F32),
            ),
            in_specs=[vmem],
            out_specs=(vmem, vmem),
        )(pltpu.with_memory_space_constraint(every, pltpu.VMEM))

    return jax.shard_map(shards, mesh=mesh, in_specs=in_specs, out_specs=out_specs, check_vma=False)
```

```python
import functools

import jax
import jax.numpy as jnp
from jax import lax
from jax.experimental import pallas as pl
from jax.experimental.pallas import tpu as pltpu
from jax.sharding import PartitionSpec as P

MESH = pl.DeviceIdType.MESH
BF = jnp.bfloat16
F32 = jnp.float32

sharpness = 4.0
max_shift = 2.0
OFF = -1e30

Q = 16
STRIDE = 17
ROWS_M = STRIDE * Q
ROWS_X = (STRIDE + 2) * Q
RING = 384


def dot(a, b, dims=((1,), (0,))):
    return lax.dot_general(a, b, (dims, ((), ())), preferred_element_type=F32)


def store_slabs(ref, index, y, low=0):
    ref[index, low : low + y.shape[0], :] = y.astype(BF)
    if low == 0:
        first = pltpu.roll(y[0:Q], Q - 1, 0)
        second = pltpu.roll(y[Q : 2 * Q], Q - 1, 0)
        ref[index, ROWS_M:ROWS_X, :] = jnp.concatenate([first, second], axis=0).astype(BF)


def kernel(
    n_rows,
    src_in,
    tgt_in,
    prior_ref,
    off_in,
    table_in,
    inw_in,
    inb_in,
    hw_ref,
    hb_in,
    outw_in,
    outb_in,
    every,
    off_ref,
    table_ref,
    inw_ref,
    inb_ref,
    hb_ref,
    outw_ref,
    outb_ref,
    img,
    side,
    own_s,
    own_t,
    pri,
    wts,
    turned,
    order,
    gin,
    toe,
    gout,
    wout,
    feat,
    hid1,
    part1,
    part2,
    sums_out,
    own_lhs,
    part_of,
    bands,
    masks,
    in_sem,
    w_sem,
    p_sem,
    img_send,
    img_recv,
    pri_send,
    pri_recv,
    cand_send,
    cand_recv,
):
    pair = lax.axis_index("pair")
    row = lax.axis_index("rows")
    col = lax.axis_index("cols")
    has_up = row > 0
    has_down = row < n_rows - 1
    up = jnp.maximum(row - 1, 0)
    down = jnp.minimum(row + 1, n_rows - 1)
    other = 1 - col
    partner = 1 - pair
    tile_rows = 8
    rows_all = n_rows * tile_rows
    places = (
        (pair, up, col),
        (pair, down, col),
        (pair, row, other),
        (pair, up, other),
        (pair, down, other),
    )

    sends_to = (has_up, has_down, None, has_up, has_down)
    comes_from = (has_down, has_up, None, has_down, has_up)

    def only_if(condition, action):
        if condition is None:
            action()
        else:
            pl.when(condition)(action)

    def signal(place):
        pl.semaphore_signal(barrier, inc=1, device_id=place, device_id_type=MESH)

    barrier = pltpu.get_barrier_semaphore()
    for number in (0, 3, 1, 4, 2):
        only_if(sends_to[number], functools.partial(signal, places[number]))
    signal((partner, row, col))

    loads = []
    for number, (source, target) in enumerate(
        (
            (src_in, own_s),
            (tgt_in, own_t),
            (inw_in, inw_ref),
            (outw_in, outw_ref),
            (off_in, off_ref),
            (table_in, table_ref),
            (inb_in, inb_ref),
            (hb_in, hb_ref),
            (outb_in, outb_ref),
        )
    ):
        copy = pltpu.make_async_copy(source, target, in_sem.at[number])
        copy.start()
        loads.append(copy)

    weight_copies = []
    for number, (a, where, r0, l0) in enumerate(
        ((0, 0, 0, 0), (1, 0, 128, 0), (0, 0, 128, 128), (2, 1, 0, 0), (1, 1, 0, 128), (2, 1, 128, 128))
    ):
        copy = pltpu.make_async_copy(
            hw_ref.at[:, pl.ds(3 * a, 3)],
            wts.at[:, :, where, pl.ds(r0, 128), pl.ds(l0, 128)],
            w_sem.at[number],
        )
        copy.start()
        weight_copies.append(copy)
    own_prior = pltpu.make_async_copy(
        prior_ref, pri.at[:, :, pl.ds(8, 8), pl.ds(0, 256)], p_sem
    )
    own_prior.start()

    for copy in loads[:2]:
        copy.wait()
    own_rows = [own_s[...], own_t[0], own_t[1]]
    own = jnp.concatenate(
        [x.astype(F32) for x in own_rows] + [jnp.zeros((8, 256), F32)], axis=0
    ).astype(BF)
    img[0, :, 0:256] = own
    side[...] = jnp.where(col == 0, own[:, 128:256], own[:, 0:128])
    for copy in loads[2:]:
        copy.wait()

    lane8 = lax.broadcasted_iota(jnp.int32, (8, RING), 1)
    sub8 = lax.broadcasted_iota(jnp.int32, (8, RING), 0)
    lanes_ok = (lane8 < 256) | ((lane8 < 320) == (col == 0))
    above_ok = jnp.logical_and(lanes_ok, has_up)
    below_ok = jnp.logical_and(lanes_ok, has_down)
    blank = jnp.zeros((8, RING), F32)

    def gather_columns(rows_of):
        three = [rows_of(s) for s in range(3)]
        space = [blank] * 4
        stack = jnp.concatenate(
            list(three[0] + three[1]) + space + list(three[0] + three[2]) + space, axis=0
        )
        turned[4 : RING + 4, :] = jnp.transpose(stack)
        turned[0:4, :] = turned[RING : RING + 4, :]
        slabs = [turned[pl.ds(i, Q, STRIDE), :] for i in range(STRIDE + 2)]
        group = lax.broadcasted_iota(jnp.int32, (ROWS_M, 128), 1) // 32
        out = []
        for k in range(2):
            moved = [
                jnp.concatenate(slabs[b : b + STRIDE], axis=0)
                if (32 * b - 64 * k) % 128 == 0
                else pltpu.roll(jnp.concatenate(slabs[b : b + STRIDE], axis=0), (32 * b - 64 * k) % 128, 1)
                for b in range(3)
            ]
            out.append(
                jnp.where(group == 0, moved[0], jnp.where(group == 1, moved[1], moved[2])).astype(BF)
            )
        return out

    def image(slot, s):
        return img[slot].astype(F32)[8 * s : 8 * s + 8]

    def own_image(s):
        return (jnp.where(lanes_ok, image(0, s), 0.0), blank)

    def own_image_alone(s):
        mine = img[0, :, 0:256].astype(F32)[8 * s : 8 * s + 8]
        return (jnp.concatenate([mine, jnp.zeros((8, 128), F32)], axis=1), blank)

    def above_rows(s):
        return (blank, jnp.where(jnp.logical_and(sub8 >= 4, above_ok), image(1, s), 0.0))

    def below_rows(s):
        return (blank, jnp.where(jnp.logical_and(sub8 < 4, below_ok), image(2, s), 0.0))

    def halo_rows(s):
        return (blank, jnp.where(sub8 < 4, below_rows(s)[1], above_rows(s)[1]))

    def row_bias(bias, first_row):
        which = first_row + lax.broadcasted_iota(jnp.int32, (1, 256), 1) // 128
        return jnp.where((which >= 0) & (which < rows_all), bias, OFF)

    def twice(vector):
        return jnp.concatenate([vector, vector], axis=1)

    def finish(total, bias, layer, low=0):
        y = jnp.maximum(total + bias, 0.0)
        if low > 0:
            return y
        count = min(7 * Q, y.shape[0])
        masked = y[0:count] * masks[layer, 0:count, :]
        return masked if count == y.shape[0] else jnp.concatenate([masked, y[count:]], axis=0)

    def first_layer(k, p, lhs):
        total = dot(lhs, toe[:, p * 256 : (p + 1) * 256])
        bias_here = row_bias(first_bias[k], row * tile_rows + 2 * p - 3)
        store_slabs(feat.at[k], p, finish(total, bias_here, 0))

    def taps(source, k, p, layer, wheres, low, count):
        total = None
        for where in wheres:
            for b in range(3):
                rows = source[k, p + where, b * Q + low : b * Q + low + count, :]
                term = dot(rows, wts[layer, b, where])
                total = term if total is None else total + term
        return total

    hidden_layers = ((feat, part1), (hid1, part2))

    def hidden(k, p, layer, wheres=(0, 1), part=None, low=0, count=ROWS_M):
        source, sums = hidden_layers[layer]
        total = taps(source, k, p, layer, wheres, low, count)
        if part is not None:
            total = total + sums[k, part]
        bias_here = row_bias(hidden_bias[layer], row * tile_rows + 2 * p - 2 + layer)
        y = finish(total, bias_here, layer + 1, low)
        if layer == 0:
            store_slabs(hid1.at[k], p, y, low)
        else:
            part_of[k, p, low : low + count, :] = y.astype(BF)

    def partial(k, p, layer, where, part, low=0, count=ROWS_M):
        source, sums = hidden_layers[layer]
        sums[k, part, low : low + count, :] = taps(source, k, p, layer, (where,), low, count)

    table = table_ref[...].astype(F32)
    in_bias = inb_ref[...].reshape(1, 128)
    hidden_bias = [twice(hb_ref[layer : layer + 1, :]) for layer in range(2)]
    first_bias = []
    for k in range(2):
        embed = jnp.zeros((1, 128), F32)
        for o in range(table.shape[0]):
            embed = embed + jnp.where(off_ref[k] == o, table[o : o + 1], 0.0)
        first_bias.append(twice(in_bias + embed))

    main = pl.ds(0, 256)
    edge = pl.ds(256, 128)
    half = pl.ds(pl.multiple_of((1 - col) * 128, 128), 128)
    routes = ((2, main), (1, main), (0, edge), (2, edge), (1, edge))
    prior_copies = []
    for number, (slot, lanes) in enumerate(routes):
        start = (8, 0, 16)[slot]
        copy = pltpu.make_async_remote_copy(
            src_ref=prior_ref if number < 2 else prior_ref.at[:, :, :, half],
            dst_ref=pri.at[:, :, pl.ds(start, 8), lanes],
            send_sem=pri_send.at[number],
            recv_sem=pri_recv.at[number],
            device_id=places[number],
            device_id_type=MESH,
        )
        prior_copies.append(copy)

    def send_priors():
        for number in range(5):
            only_if(sends_to[number], prior_copies[number].start)

    def make_constants():
        order[...] = jnp.zeros_like(order)

        m_slab = lax.broadcasted_iota(jnp.int32, (7, Q, 256), 0)
        m_chunk = lax.broadcasted_iota(jnp.int32, (7, Q, 256), 1)
        m_at = m_chunk * STRIDE + m_slab + col * 256
        for layer in range(3):
            inside = (m_at >= 3 - layer) & (m_at < 512 + 3 - layer)
            masks[layer] = jnp.where(inside, 1.0, 0.0).reshape(7 * Q, 256)

        gin[...] = jnp.zeros_like(gin)
        for b in range(3):
            for ch in range(2):
                for a in range(3):
                    w = inw_ref[3 * a + b, ch : ch + 1, :].astype(F32)
                    gin[2 * b + ch, a : a + 1, :] = w
                    gin[2 * b + ch, 16 + a : 17 + a, :] = w
        for r in range(14):
            start = (20 - r) % 16
            block = jnp.concatenate(
                [gin[g, start : start + 16, :] for g in range(6)] + [jnp.zeros((32, 128), F32)], axis=0
            )
            toe[:, r * 128 : (r + 1) * 128] = block.astype(BF)

        gout[...] = jnp.zeros_like(gout)
        for b in range(3):
            for e in range(2):
                for a in range(3):
                    gout[2 * b + e, 10 - a : 11 - a, :] = outw_ref[3 * a + b, e : e + 1, :].astype(F32)
        for p in range(5):
            for h in range(2):
                start = 10 - (2 * p + h)
                block = jnp.concatenate(
                    [gout[g, start : start + 8, :] for g in range(6)] + [jnp.zeros((80, 128), F32)], axis=0
                )
                wout[p, h * 128 : (h + 1) * 128, :] = jnp.transpose(block).astype(BF)

        for layer in range(2):
            for b in range(3):
                wts[layer, b, 0, 0:128, 128:256] = jnp.zeros((128, 128), BF)
                wts[layer, b, 1, 128:256, 0:128] = jnp.zeros((128, 128), BF)


    def own_first(rows_of):
        columns = gather_columns(rows_of)
        for k in range(2):
            own_lhs[k] = columns[k]
            for p in (2, 3, 4):
                first_layer(k, p, columns[k])

    def own_hidden(first_ranges, second_ranges):
        for low, count in first_ranges:
            for k in range(2):
                for p in (2, 3):
                    hidden(k, p, 0, low=low, count=count)
            for k in range(2):
                partial(k, 1, 0, 1, 0, low, count)
                partial(k, 4, 0, 0, 1, low, count)
        for low, count in second_ranges:
            for k in range(2):
                hidden(k, 2, 1, low=low, count=count)
            for k in range(2):
                partial(k, 1, 1, 1, 0, low, count)
                partial(k, 3, 1, 0, 1, low, count)
        for low, count in second_ranges:
            for k in range(2):
                sums_out[k, low : low + count, :] = dot(part_of[k, 2, low : low + count, :], wout[2])

    def wait_weights():
        for copy in weight_copies:
            copy.wait()

    whole = ((0, ROWS_M),)
    early = jnp.logical_and(row % 8 == 0, jnp.logical_and(row != 0, row != n_rows // 2))

    @pl.when(early)
    def _():
        make_constants()
        own_first(own_image_alone)
        wait_weights()
        own_hidden(whole, whole)

    pl.semaphore_wait(barrier, 2 + 2 * has_up.astype(jnp.int32) + 2 * has_down.astype(jnp.int32))

    image_copies = [None] * 5
    for number in (2, 0, 3, 1, 4):
        slot, lanes = routes[number]
        copy = pltpu.make_async_remote_copy(
            src_ref=img.at[0, :, main] if number < 2 else side,
            dst_ref=img.at[slot, :, lanes],
            send_sem=img_send.at[number],
            recv_sem=img_recv.at[number],
            device_id=places[number],
            device_id_type=MESH,
        )
        only_if(sends_to[number], copy.start)
        image_copies[number] = copy

    @pl.when(early)
    def _():
        send_priors()
        image_copies[2].wait_recv()
        own_first(own_image)
        own_hidden(((0, 5 * Q),), ((0, 4 * Q), (16 * Q, Q)))

    @pl.when(jnp.logical_not(early))
    def _():
        make_constants()
        image_copies[2].wait_recv()
        own_first(own_image)
        send_priors()
        wait_weights()
        own_hidden(whole, whole)

    def shift_priors():
        for number in range(5):
            only_if(comes_from[number], prior_copies[number].wait_recv)
        own_prior.wait()
        for k in range(2):
            for e in range(2):
                pri[k, e, 0:8, :] = jnp.where(above_ok, pri[k, e, 0:8, :], 0.0)
                pri[k, e, 8:16, :] = jnp.where(lanes_ok, pri[k, e, 8:16, :], 0.0)
                pri[k, e, 16:24, :] = jnp.where(below_ok, pri[k, e, 16:24, :], 0.0)
                for rs in range(5):
                    band = pri[k, e, 6 + rs : 14 + rs, :]
                    for cs in range(5):
                        moved = band if cs == 2 else pltpu.roll(band, (RING + 2 - cs) % RING, 1)
                        bands[k, e, rs, cs] = moved[:, 0:256]

    def outer(rows_of, sides, arrivals, then=None):
        for number in arrivals:
            only_if(comes_from[number], image_copies[number].wait_recv)
        more = gather_columns(rows_of)
        for k in range(2):
            lhs = own_lhs[k] + more[k]
            for side_of in sides:
                for p in ((0, 1), (5, 6))[side_of]:
                    first_layer(k, p, lhs)
        for k in range(2):
            for side_of in sides:
                hidden(k, (0, 5)[side_of], 0)
                hidden(k, (1, 4)[side_of], 0, (side_of,), side_of)
        if then is not None:
            then()
        for k in range(2):
            for side_of in sides:
                hidden(k, (0, 4)[side_of], 1)
                hidden(k, (1, 3)[side_of], 1, (side_of,), side_of)
        for k in range(2):
            total = sums_out[k]
            for side_of in sides:
                for p in ((0, 1), (4, 3))[side_of]:
                    total = total + dot(part_of[k, p], wout[p])
            sums_out[k] = total

    middle = n_rows // 2
    below_first = jnp.logical_or(row == middle, jnp.logical_and(row % 8 == 1, row > 1))
    above_first = row == middle - 1

    @pl.when(below_first)
    def _():
        outer(below_rows, (1,), (0, 3))
        outer(above_rows, (0,), (1, 4), shift_priors)

    @pl.when(above_first)
    def _():
        outer(above_rows, (0,), (1, 4))
        outer(below_rows, (1,), (0, 3), shift_priors)

    @pl.when(jnp.logical_not(jnp.logical_or(below_first, above_first)))
    def _():
        outer(halo_rows, (0, 1), (0, 1, 3, 4), shift_priors)

    for k in range(2):
        for i in range(STRIDE):
            order[k, pl.ds(i, Q, STRIDE), :] = sums_out[k, i * Q : (i + 1) * Q, :]
        natural = jnp.transpose(order[k])
        flow = []
        for e in range(2):
            z0 = natural[8 * e : 8 * e + 8]
            z1 = pltpu.roll(natural[16 + 8 * e : 24 + 8 * e], RING - 1, 1)
            z2 = pltpu.roll(natural[32 + 8 * e : 40 + 8 * e], RING - 2, 1)
            flow.append(max_shift * jnp.tanh((z0 + z1 + z2)[:, 0:256] + outb_ref[e]))
        row_weight = [jnp.maximum(1.0 - jnp.abs(flow[0] - s), 0.0) for s in range(-2, 3)]
        col_weight = [jnp.maximum(1.0 - jnp.abs(flow[1] - s), 0.0) for s in range(-2, 3)]
        mine = pair * 2 + k
        for e in range(2):
            value = flow[e]
            for rs in range(5):
                inner = None
                for cs in range(5):
                    term = col_weight[cs] * bands[k, e, rs, cs]
                    inner = term if inner is None else inner + term
                value = value + row_weight[rs] * inner
            every[mine, e] = value
        copy = pltpu.make_async_remote_copy(
            src_ref=every.at[mine],
            dst_ref=every.at[mine],
            send_sem=cand_send.at[k],
            recv_sem=cand_recv.at[k],
            device_id=(partner, row, col),
            device_id_type=MESH,
        )
        copy.start()
        if k == 0:
            first_copy = copy
        else:
            second_copy = copy

    first_copy.wait()
    second_copy.wait()
    for number in range(5):
        only_if(sends_to[number], image_copies[number].wait_send)
        only_if(sends_to[number], prior_copies[number].wait_send)


def vote(every, cand_ref, vote_ref):
    pair = lax.axis_index("pair")
    for k in range(2):
        cand_ref[k] = every[2 * pair + k]
    c = [[every[k, e] for e in range(2)] for k in range(4)]
    score = [None] * 4
    for i in range(4):
        for j in range(i + 1, 4):
            dr = c[i][0] - c[j][0]
            dc = c[i][1] - c[j][1]
            apart = dr * dr + dc * dc
            score[i] = apart if score[i] is None else score[i] + apart
            score[j] = apart if score[j] is None else score[j] + apart
    weight = [jnp.exp(score[i] * (-1.0 / (3 * sharpness))) for i in range(4)]
    bottom = (weight[0] + weight[1]) + (weight[2] + weight[3])
    for e in range(2):
        top = (weight[0] * c[0][e] + weight[1] * c[1][e]) + (
            weight[2] * c[2][e] + weight[3] * c[3][e]
        )
        vote_ref[e] = top / bottom


def solution(mesh):
    n_rows = mesh.shape["rows"]
    in_specs = (
        P("rows", "cols"),
        P("pair", "rows", "cols"),
        P("pair", None, "rows", "cols"),
        P("pair"),
        P(),
        P(),
        P(),
        P(),
        P(),
        P(),
        P(),
    )
    out_specs = (P("pair", None, "rows", "cols"), P(None, "rows", "cols"))
    vmem = pl.BlockSpec(memory_space=pltpu.VMEM)
    hbm = pl.BlockSpec(memory_space=pltpu.HBM)
    dma = pltpu.SemaphoreType.DMA

    def shards(*args):
        args = [pltpu.with_memory_space_constraint(x, pltpu.HBM) for x in args]
        every = pl.pallas_call(
            functools.partial(kernel, n_rows),
            out_shape=pltpu.VMEM((4, 2, 8, 256), F32),
            in_specs=[hbm] * 11,
            out_specs=vmem,
            scratch_shapes=[
                pltpu.SMEM((2,), jnp.int32),
                pltpu.VMEM((3, 128), BF),
                pltpu.VMEM((9, 2, 128), BF),
                pltpu.VMEM((128,), F32),
                pltpu.VMEM((2, 128), F32),
                pltpu.VMEM((9, 2, 128), BF),
                pltpu.SMEM((2,), F32),
                pltpu.VMEM((3, 32, RING), BF),
                pltpu.VMEM((32, 128), BF),
                pltpu.VMEM((8, 256), BF),
                pltpu.VMEM((2, 8, 256), BF),
                pltpu.VMEM((2, 2, 24, RING), F32),
                pltpu.VMEM((2, 3, 2, 256, 256), BF),
                pltpu.VMEM((RING + 8, 128), F32),
                pltpu.VMEM((2, RING, 128), F32),
                pltpu.VMEM((6, 32, 128), F32),
                pltpu.VMEM((128, 14 * 128), BF),
                pltpu.VMEM((6, 24, 128), F32),
                pltpu.VMEM((5, 256, 128), BF),
                pltpu.VMEM((2, 7, ROWS_X, 256), BF),
                pltpu.VMEM((2, 6, ROWS_X, 256), BF),
                pltpu.VMEM((2, 2, ROWS_M, 256), F32),
                pltpu.VMEM((2, 2, ROWS_M, 256), F32),
                pltpu.VMEM((2, ROWS_M, 128), F32),
                pltpu.VMEM((2, ROWS_M, 128), BF),
                pltpu.VMEM((2, 5, ROWS_M, 256), BF),
                pltpu.VMEM((2, 2, 5, 5, 8, 256), F32),
                pltpu.VMEM((3, 7 * Q, 256), F32),
                dma((9,)),
                dma((6,)),
                dma,
                dma((5,)),
                dma((5,)),
                dma((5,)),
                dma((5,)),
                dma((2,)),
                dma((2,)),
            ],
            compiler_params=pltpu.CompilerParams(
                collective_id=0, has_side_effects=True, vmem_limit_bytes=40 * 1024 * 1024
            ),
        )(*args)
        return pl.pallas_call(
            vote,
            out_shape=(
                jax.ShapeDtypeStruct((2, 2, 8, 256), F32),
                jax.ShapeDtypeStruct((2, 8, 256), F32),
            ),
            in_specs=[vmem],
            out_specs=(vmem, vmem),
        )(pltpu.with_memory_space_constraint(every, pltpu.VMEM))

    return jax.shard_map(shards, mesh=mesh, in_specs=in_specs, out_specs=out_specs, check_vma=False)
```
